256 devices in a mesh: gx: 4 (over y), gy: 8 (over z), gz: 8 (over x, core).
Axes of the slice: x: 4, y: 4, z: 8, core: 2. Of those that a mesh axis runs over, the one named last changes fastest.
Arguments:
- previous: float32 [16, 32, 128, 1024], P(None, 'gx', 'gy', 'gz'), may hold values from -6 to 6
- current: float32 [16, 32, 128, 1024], P(None, 'gx', 'gy', 'gz'), may hold values from -6 to 6
- potential: float32 [32, 128, 1024], P('gx', 'gy', 'gz'), may hold values from -1 to 1
- projector: float32 [4, 8, 8, 27, 4, 18, 128], P('gx', 'gy', 'gz'), may hold values from -0.3 to 0.3
- node_index: int32 [4, 8, 8, 27, 4, 128], P('gx', 'gy', 'gz'), may hold values from 0 to 16383
- coupling: float32 [1024, 18, 18], P(('gx', 'gy', 'gz')), may hold values from -1.5 to 1.5
- cut_low: float32 [1], replicated, may hold values from 0.5 to 1.5
- cut_high: float32 [1], replicated, may hold values from 8 to 10
Outputs:
- next_field: float32 [16, 32, 128, 1024], P(None, 'gx', 'gy', 'gz')
- last_field: float32 [16, 32, 128, 1024], P(None, 'gx', 'gy', 'gz')
The draws below stay inside these ranges and needn't reach their ends.
Inputs may be any that keep to these rules, and one draw needn't show every extreme that they name: `node_index`: local node numbers of a device's block, x slowest and z fastest.
All inputs are finite; a program needn't handle non-finite values.
Results may differ from the reference program's by a relative error of at most 0.00005.
Values sent between devices are 32-bit elements; how exact they have to be, the bound alone decides.
A program may use at most 128 MiB of HBM per device.

```python
import jax
import jax.numpy as jnp
from jax import lax

BANDS = 16
NPROJ = 18
CX = 8
CY = 16
CZ = 128
ATOM_DEV = 4
SUP = 128
NX = 32
NY = 128
NZ = 1024
ATOMS = 1024
N_GX = 4
N_GY = 8
N_GZ = 8


def with_ends(values, stream_key, least, largest):
    longest = values.shape.index(max(values.shape))
    spots = []
    for shift in (0, 1):
        where = [jax.random.randint(jax.random.fold_in(stream_key, axis), (), 0, length) for axis, length in enumerate(values.shape)]
        where[longest] = (where[longest] + shift) % values.shape[longest]
        spots.append(tuple(where))
    return values.at[spots[0]].set(least).at[spots[1]].set(largest)


def block_levels(key, extent, cuts, low, high):
    loudness, own = 1.0, jax.random.fold_in(key, 6)
    for axis_at, blocks in cuts:
        steps = jnp.exp(jax.random.uniform(jax.random.fold_in(own, axis_at), (blocks,), jnp.float32, low / len(cuts), high / len(cuts)))
        loudness = loudness * jnp.repeat(steps, extent[axis_at] // blocks).reshape([-1 if axis == axis_at else 1 for axis in range(len(extent))])
    return loudness


def gaussian(own_key, dims, scale, bound, cuts=(), kind=jnp.bfloat16):
    drawn = jax.random.normal(own_key, dims, jnp.float32) * scale
    if len(cuts) > 0:
        drawn = block_levels(own_key, dims, cuts, -0.22, 0.18) * drawn
    return jnp.clip(drawn, min=-bound, max=bound).astype(kind)


def setup_inputs(seed: int = 0) -> dict:
    arg_keys = jax.random.split(jax.random.key(seed), 9)
    return {
        "previous": gaussian(arg_keys[0], (BANDS, NX, NY, NZ), 1.0, 6.0, ((1, 4), (2, 8), (3, 8)), jnp.float32),
        "current": gaussian(arg_keys[1], (BANDS, NX, NY, NZ), 1.0, 6.0, ((1, 4), (2, 8), (3, 8)), jnp.float32),
        "potential": jnp.clip(jax.random.uniform(arg_keys[2], (NX, NY, NZ), jnp.float32, -1.0, 1.0) * block_levels(arg_keys[2], (NX, NY, NZ), ((0, 4), (1, 8), (2, 8)), -0.4, 0.0), -1.0, 1.0),
        "projector": gaussian(arg_keys[3], (N_GX, N_GY, N_GZ, 27, ATOM_DEV, NPROJ, SUP), 0.05, 0.3, ((0, 4), (1, 8), (2, 8)), jnp.float32),
        "node_index": with_ends(jax.random.randint(arg_keys[4], (N_GX, N_GY, N_GZ, 27, ATOM_DEV, SUP), 0, CX * CY * CZ), jax.random.fold_in(arg_keys[4], 1), 0, (CX * CY * CZ) - 1).astype(jnp.int32),
        "coupling": gaussian(arg_keys[5], (ATOMS, NPROJ, NPROJ), NPROJ ** -0.5, 1.5, ((0, 256),), jnp.float32),
        "cut_low": jnp.clip(jax.random.uniform(arg_keys[6], (1,), jnp.float32, 0.5, 1.5), 0.5, 1.5),
        "cut_high": jnp.clip(jax.random.uniform(arg_keys[7], (1,), jnp.float32, 8.0, 10.0), 8.0, 10.0),
    }


def reference(previous, current, potential, projector, node_index, coupling, cut_low, cut_high):
    centre = 0.5 * (cut_high[0] + cut_low[0])
    radius = 0.5 * (cut_high[0] - cut_low[0])
    device_x = jnp.arange(N_GX, dtype=jnp.int32)[:, None, None, None, None, None]
    device_y = jnp.arange(N_GY, dtype=jnp.int32)[None, :, None, None, None, None]
    device_z = jnp.arange(N_GZ, dtype=jnp.int32)[None, None, :, None, None, None]
    global_x = (device_x * CX + node_index // (CY * CZ)).reshape(-1, SUP)
    global_y = (device_y * CY + (node_index // CZ) % CY).reshape(-1, SUP)
    global_z = (device_z * CZ + node_index % CZ).reshape(-1, SUP)
    offsets = jnp.arange(27, dtype=jnp.int32)[None, None, None, :, None]
    owner_x = device_x[..., 0] + offsets // 9 - 1
    owner_y = device_y[..., 0] + (offsets // 3) % 3 - 1
    owner_z = device_z[..., 0] + offsets % 3 - 1
    inside = (owner_x >= 0) & (owner_x < N_GX) & (owner_y >= 0) & (owner_y < N_GY) & (owner_z >= 0) & (owner_z < N_GZ)
    slot_ids = jnp.arange(ATOM_DEV, dtype=jnp.int32)[None, None, None, None, :]
    atom_id = jnp.where(inside, ((owner_x * N_GY + owner_y) * N_GZ + owner_z) * ATOM_DEV + slot_ids, ATOMS)
    atom_id = atom_id.reshape(-1).astype(jnp.int32)
    proj_rows = projector.reshape(-1, NPROJ, SUP)

    def apply_hamiltonian(values_in):
        padded = jnp.pad(values_in, ((0, 0), (1, 1), (1, 1), (1, 1)))
        beside = padded[:, 2:, 1:-1, 1:-1] + padded[:, :-2, 1:-1, 1:-1]
        beside = beside + padded[:, 1:-1, 2:, 1:-1] + padded[:, 1:-1, :-2, 1:-1]
        beside = beside + padded[:, 1:-1, 1:-1, 2:] + padded[:, 1:-1, 1:-1, :-2]
        kinetic = 0.5 * (6.0 * values_in - beside)

        def band_partial(band_field):
            picked = band_field[global_x, global_y, global_z]
            return jnp.einsum('nps,ns->np', proj_rows, picked, precision=lax.Precision.HIGHEST)

        partial_value = jnp.transpose(lax.map(band_partial, values_in), (1, 2, 0))
        coefficient = jax.ops.segment_sum(partial_value, atom_id, num_segments=ATOMS + 1)[:ATOMS]
        weighted = jnp.einsum('apq,aqb->apb', coupling, coefficient, precision=lax.Precision.HIGHEST)
        weighted = jnp.concatenate([weighted, jnp.zeros((1, NPROJ, BANDS), jnp.float32)], 0)[atom_id]

        def band_back(band_weights):
            spread = jnp.einsum('nps,np->ns', proj_rows, band_weights, precision=lax.Precision.HIGHEST)
            return jnp.zeros((NX, NY, NZ), jnp.float32).at[global_x, global_y, global_z].add(spread)

        projected = lax.map(band_back, jnp.transpose(weighted, (2, 0, 1)))
        return kinetic + potential[None] * values_in + projected

    next_field = (2.0 / radius) * (apply_hamiltonian(current) - centre * current) - previous
    last_field = (2.0 / radius) * (apply_hamiltonian(next_field) - centre * next_field) - current
    return next_field, last_field
```

```python
import jax
import jax.numpy as jnp
from jax import lax
from jax.experimental import pallas as pl
from jax.experimental.pallas import tpu as pltpu
from jax.sharding import PartitionSpec as P

F32 = jnp.float32
BF16 = jnp.bfloat16
MESH = pl.DeviceIdType.MESH

BANDS = 16
ROWS = 128
LANES = 128
LINE = 16
PLANES = 8
NOFF = 27
ATOMS = 4
NPROJ = 18
PPAD = 32
PSEND = 24
NBLK = NOFF * ATOMS
HALF = ROWS // 2
CENTRE = NOFF // 2
NGROUP = (NOFF + 1) // 2


def split(value):
    high = value.astype(BF16)
    return high, (value - high.astype(F32)).astype(BF16)


def kernel(
    sizes,
    index_s, low_s, high_s,
    previous, current, potential, projector, index_v, coupling,
    following, last,
    table, onehot, proj_hi, proj_lo, gathered, coup,
    send_c, recv_c, send_w, recv_w,
    face_y, face_z, halo_x, halo_y, halo_z,
    sem_sc, sem_rc, sem_sw, sem_rw, sem_sh, sem_rh,
):
    place = tuple(lax.axis_index(axis) for axis in ("gx", "gy", "gz"))
    centre = 0.5 * (high_s[0] + low_s[0])
    radius = 0.5 * (high_s[0] - low_s[0])
    scale = 2.0 / radius

    def shift_of(offset):
        return offset // 9 - 1, (offset // 3) % 3 - 1, offset % 3 - 1

    def wrapped(shift, sign):
        return tuple(
            lax.rem(at + sign * step + count, count)
            for at, step, count in zip(place, shift, sizes)
        )

    def inside(shift, sign):
        valid = None
        for at, step, count in zip(place, shift, sizes):
            there = at + sign * step
            here = (there >= 0) & (there < count)
            valid = here if valid is None else valid & here
        return valid

    barrier = pltpu.get_barrier_semaphore()

    def greet(offset, carry):
        @pl.when(offset != CENTRE)
        def _():
            pl.semaphore_signal(
                barrier, inc=1, device_id=wrapped(shift_of(offset), 1), device_id_type=MESH
            )
        return carry

    lax.fori_loop(0, NOFF, greet, 0)

    lane = lax.broadcasted_iota(jnp.int32, (8, LANES), 1)
    sub = lax.broadcasted_iota(jnp.int32, (8, LANES), 0)
    lane_of = lambda rows: lax.broadcasted_iota(jnp.int32, (rows, LANES), 1)
    row_of = lambda rows: lax.broadcasted_iota(jnp.int32, (rows, LANES), 0)

    def halves(block, carry):
        values = jnp.concatenate(
            [projector[block], jnp.zeros((PPAD - NPROJ, LANES), F32)], axis=0
        )
        high, low = split(values)
        at = pl.ds(pl.multiple_of(block * PPAD, PPAD), PPAD)
        proj_hi[at, :] = high
        proj_lo[at, :] = low
        return carry

    lax.fori_loop(0, NBLK, halves, 0)
    tail = pl.ds(NBLK * PPAD, (2 * NGROUP - NOFF) * ATOMS * PPAD)
    proj_hi[tail, :] = jnp.zeros((ATOMS * PPAD, LANES), BF16)
    proj_lo[tail, :] = jnp.zeros((ATOMS * PPAD, LANES), BF16)

    coup[...] = jnp.zeros(coup.shape, F32)
    for atom in range(ATOMS):
        coup[atom * PPAD:atom * PPAD + NPROJ, 0:NPROJ] = coupling[atom]

    def hot(block, carry):
        node = index_v[pl.ds(block, 1), :]
        column = (node // (HALF * LANES)) * LANES + node % LANES
        wide = lax.broadcasted_iota(jnp.int32, (2 * LANES, LANES), 0)
        onehot[:, pl.ds(pl.multiple_of(block * LANES, LANES), LANES)] = jnp.where(
            wide == column, 1.0, 0.0
        ).astype(BF16)
        return carry

    lax.fori_loop(0, NBLK, hot, 0)

    pl.semaphore_wait(barrier, NOFF - 1)

    sides = [(axis, sign) for axis in range(3) for sign in (1, -1)]

    def neighbour(axis, sign):
        return tuple(
            lax.rem(at + sign + sizes[n], sizes[n]) if n == axis else at
            for n, at in enumerate(place)
        )

    def halo_copies(step, field):
        copies = []
        for n, (axis, sign) in enumerate(sides):
            slot = 0 if sign == 1 else 1
            if axis == 0:
                source = field.at[:, pl.ds(ROWS - LINE if sign == 1 else 0, LINE), :]
                target = halo_x.at[step, slot]
            elif axis == 1:
                source, target = face_y.at[step, slot], halo_y.at[step, slot]
            else:
                source, target = face_z.at[step, slot], halo_z.at[step, slot]
            copies.append(
                pltpu.make_async_remote_copy(
                    src_ref=source, dst_ref=target,
                    send_sem=sem_sh.at[step, n], recv_sem=sem_rh.at[step, n],
                    device_id=neighbour(axis, sign), device_id_type=MESH,
                )
            )
        return copies

    def part_copy(step, offset):
        return pltpu.make_async_remote_copy(
            src_ref=send_c.at[step, offset // 2], dst_ref=recv_c.at[step, offset],
            send_sem=sem_sc.at[step, offset], recv_sem=sem_rc.at[step, offset],
            device_id=wrapped(shift_of(offset), 1), device_id_type=MESH,
        )

    def weight_copy(step, offset):
        return pltpu.make_async_remote_copy(
            src_ref=send_w.at[step], dst_ref=recv_w.at[step, offset],
            send_sem=sem_sw.at[step, offset], recv_sem=sem_rw.at[step, offset],
            device_id=wrapped(shift_of(offset), -1), device_id_type=MESH,
        )

    def advance(step, before, field, result):
        face_y[step, 0] = field[:, pl.ds(LINE - 1, PLANES, stride=LINE), :]
        face_y[step, 1] = field[:, pl.ds(0, PLANES, stride=LINE), :]
        top = jnp.zeros((ROWS, LANES), F32)
        bottom = jnp.zeros((ROWS, LANES), F32)
        lanes = lane_of(ROWS)
        for band in range(BANDS):
            plane = field[band]
            top = jnp.where(lanes == band, pltpu.roll(plane, band + 1, 1), top)
            bottom = jnp.where(
                lanes == band, pltpu.roll(plane, band, 1) if band else plane, bottom
            )
        face_z[step, 0] = top
        face_z[step, 1] = bottom
        halos = halo_copies(step, field)
        for copy in halos:
            copy.start()

        def turn(tile, carry):
            rows = field[:, pl.ds(pl.multiple_of(tile * 8, 8), 8), :]
            rows = jnp.swapaxes(rows, 0, 1)
            for n in range(8):
                wide = jnp.concatenate([rows[n]] * 8, axis=0)
                at = pl.ds(pl.multiple_of((tile * 8 + n) * LANES, LANES), LANES)
                table[at, :] = wide.T
            return carry

        lax.fori_loop(0, ROWS // 8, turn, 0)

        def group(g, carry):
            def pick(t, inner):
                base = [
                    jnp.minimum(g * 8 + k, NBLK - 1) * LANES + t * 8 for k in range(8)
                ]
                packed = None
                for s in range(8):
                    line = None
                    for k in range(8):
                        node = index_s[base[k] + s]
                        row = jnp.broadcast_to(table[pl.ds(node, 1), :], (8, LANES))
                        line = row if line is None else jnp.where(lane // BANDS == k, row, line)
                    packed = line if packed is None else jnp.where(sub == s, line, packed)
                gathered[pl.ds(pl.multiple_of(t * 8, 8), 8), :] = packed
                return inner

            lax.fori_loop(0, LANES // 8, pick, 0)
            high, low = split(gathered[...])
            at = pl.ds(pl.multiple_of(g * 8 * PPAD, 8 * PPAD), 8 * PPAD)
            p_hi, p_lo = proj_hi[at, :], proj_lo[at, :]
            product = jnp.dot(
                jnp.concatenate([p_hi, p_lo, p_hi], axis=1),
                jnp.concatenate([high, high, low], axis=0),
                preferred_element_type=F32,
            )
            message = jnp.zeros((PSEND, LANES), F32)
            for k in range(8):
                message = jnp.where(
                    lane_of(PSEND) // BANDS == k,
                    product[k * PPAD:k * PPAD + PSEND], message,
                )
            send_c[step, g] = message
            for odd in range(2):
                offset = g * 2 + odd

                @pl.when((offset != CENTRE) & (offset < NOFF))
                def _():
                    part_copy(step, offset).start()
            return carry

        lax.fori_loop(0, NGROUP, group, 0)

        for copy in halos:
            copy.wait()
        edge = [
            (place[axis] > 0, place[axis] < sizes[axis] - 1) for axis in range(3)
        ]
        zside = [
            jnp.where(edge[2][slot], halo_z[step, slot], 0.0) for slot in range(2)
        ]

        line_of = lax.broadcasted_iota(jnp.int32, (PLANES, LINE, LANES), 1)
        for band in range(BANDS):
            plane = field[band]
            below_x = jnp.where(edge[0][0], halo_x[step, 0, band], 0.0)
            above_x = jnp.where(edge[0][1], halo_x[step, 1, band], 0.0)
            beside = jnp.concatenate([below_x, plane[:ROWS - LINE]], axis=0)
            beside = beside + jnp.concatenate([plane[LINE:], above_x], axis=0)
            below_y = jnp.where(edge[1][0], halo_y[step, 0, band], 0.0)
            above_y = jnp.where(edge[1][1], halo_y[step, 1, band], 0.0)
            down = pltpu.roll(plane, 1, 0).reshape(PLANES, LINE, LANES)
            up = pltpu.roll(plane, ROWS - 1, 0).reshape(PLANES, LINE, LANES)
            down = jnp.where(line_of == 0, below_y[:, None, :], down)
            up = jnp.where(line_of == LINE - 1, above_y[:, None, :], up)
            beside = beside + (down + up).reshape(ROWS, LANES)
            back = pltpu.roll(plane, 1, 1)
            ahead = pltpu.roll(plane, LANES - 1, 1)
            side_b = pltpu.roll(zside[0], (LANES - band) % LANES, 1) if band else zside[0]
            side_a = pltpu.roll(zside[1], LANES - 1 - band, 1)
            back = jnp.where(lanes == 0, side_b, back)
            ahead = jnp.where(lanes == LANES - 1, side_a, ahead)
            beside = beside + (back + ahead)
            local = 0.5 * (6.0 * plane - beside) + (potential[...] - centre) * plane
            result[band] = scale * local - before[band]

        def collect(offset, total):
            @pl.when(offset != CENTRE)
            def _():
                part_copy(step, offset).wait()

            @pl.when(offset == CENTRE)
            def _():
                recv_c[step, CENTRE] = send_c[step, CENTRE // 2]

            usable = inside(shift_of(offset), -1)
            part = jnp.where(usable, recv_c[step, offset], 0.0)
            odd = lax.rem(offset, 2)
            part = jnp.where(lane_of(PSEND) // (LANES // 2) == odd, part, 0.0)
            return total + part

        total = lax.fori_loop(0, NOFF, collect, jnp.zeros((PSEND, LANES), F32))
        total = total + pltpu.roll(total, LANES // 2, 1)
        total = jnp.concatenate([total, jnp.zeros((LANES - PSEND, LANES), F32)], axis=0)
        product = jnp.dot(
            coup[...], total, precision=lax.Precision.HIGHEST, preferred_element_type=F32
        )
        weighted = jnp.zeros((PSEND, LANES), F32)
        for atom in range(ATOMS):
            weighted = jnp.where(
                (lane_of(PSEND) // BANDS) % ATOMS == atom,
                product[atom * PPAD:atom * PPAD + PSEND], weighted,
            )
        send_w[step] = scale * weighted
        recv_w[step, CENTRE] = scale * weighted

        def share(offset, carry):
            @pl.when(offset != CENTRE)
            def _():
                weight_copy(step, offset).start()
            return carry

        lax.fori_loop(0, NOFF, share, 0)

        def scatter(turn_at, carry):
            chunk = lax.rem(turn_at + 4, 9)
            parts_hi, parts_lo = [], []
            for n in range(3):
                offset = chunk * 3 + n

                @pl.when(offset != CENTRE)
                def _():
                    weight_copy(step, offset).wait()

                usable = inside(shift_of(offset), 1)
                weights = jnp.where(usable, recv_w[step, offset], 0.0)
                weights = jnp.concatenate(
                    [weights, jnp.zeros((PPAD - PSEND, LANES), F32)], axis=0
                )
                weights = jnp.concatenate([weights] * ATOMS, axis=0).T[:ATOMS * BANDS]
                keep = row_of(ATOMS * BANDS) // BANDS == lane_of(ATOMS * BANDS) // PPAD
                high, low = split(jnp.where(keep, weights, 0.0))
                at = pl.ds(pl.multiple_of(offset * ATOMS * PPAD, ATOMS * PPAD), ATOMS * PPAD)
                p_hi, p_lo = proj_hi[at, :], proj_lo[at, :]
                spread = jnp.dot(
                    jnp.concatenate([high, low, high], axis=1),
                    jnp.concatenate([p_hi, p_hi, p_lo], axis=0),
                    preferred_element_type=F32,
                )
                high, low = split(spread)
                for atom in range(ATOMS):
                    node = index_v[pl.ds(offset * ATOMS + atom, 1), :]
                    mask = (node // LANES) % HALF == row_of(HALF)
                    for value, parts in ((high, parts_hi), (low, parts_lo)):
                        mine = value[atom * BANDS:(atom + 1) * BANDS].astype(F32)
                        parts.append(
                            jnp.where(mask[None], mine[:, None, :], 0.0)
                            .astype(BF16).reshape(BANDS * HALF, LANES)
                        )
            width = 3 * ATOMS * LANES
            columns = onehot[:, pl.ds(pl.multiple_of(chunk * width, width), width)]
            product = lax.dot_general(
                jnp.concatenate(parts_hi + parts_lo, axis=1),
                jnp.concatenate([columns, columns], axis=1),
                (((1,), (1,)), ((), ())),
                preferred_element_type=F32,
            )
            product = product.reshape(BANDS, HALF, 2 * LANES)
            result[:, 0:HALF, :] += product[:, :, 0:LANES]
            result[:, HALF:ROWS, :] += product[:, :, LANES:]
            return carry

        lax.fori_loop(0, 9, scatter, 0)

    advance(0, previous, current, following)
    advance(1, current, following, last)


def shards(previous, current, potential, projector, node_index, coupling, cut_low, cut_high):
    sizes = tuple(lax.axis_size(axis) for axis in ("gx", "gy", "gz"))
    shape = current.shape
    block = (BANDS, ROWS, LANES)
    vmem = pl.BlockSpec(memory_space=pltpu.VMEM)
    smem = pl.BlockSpec(memory_space=pltpu.SMEM)
    index = node_index.reshape(-1)
    padded = 2 * NGROUP * ATOMS * PPAD

    def body(*refs):
        kernel(sizes, *refs)

    following, last = pl.pallas_call(
        body,
        out_shape=[jax.ShapeDtypeStruct(block, F32)] * 2,
        in_specs=[smem] * 3 + [vmem] * 6,
        out_specs=[vmem, vmem],
        scratch_shapes=[
            pltpu.VMEM((ROWS * LANES, LANES), F32),
            pltpu.VMEM((2 * LANES, NBLK * LANES), BF16),
            pltpu.VMEM((padded, LANES), BF16),
            pltpu.VMEM((padded, LANES), BF16),
            pltpu.VMEM((LANES, LANES), F32),
            pltpu.VMEM((ATOMS * PPAD, LANES), F32),
            pltpu.VMEM((2, NGROUP, PSEND, LANES), F32),
            pltpu.VMEM((2, NOFF, PSEND, LANES), F32),
            pltpu.VMEM((2, PSEND, LANES), F32),
            pltpu.VMEM((2, NOFF, PSEND, LANES), F32),
            pltpu.VMEM((2, 2, BANDS, PLANES, LANES), F32),
            pltpu.VMEM((2, 2, ROWS, LANES), F32),
            pltpu.VMEM((2, 2, BANDS, LINE, LANES), F32),
            pltpu.VMEM((2, 2, BANDS, PLANES, LANES), F32),
            pltpu.VMEM((2, 2, ROWS, LANES), F32),
            pltpu.SemaphoreType.DMA((2, NOFF)),
            pltpu.SemaphoreType.DMA((2, NOFF)),
            pltpu.SemaphoreType.DMA((2, NOFF)),
            pltpu.SemaphoreType.DMA((2, NOFF)),
            pltpu.SemaphoreType.DMA((2, 6)),
            pltpu.SemaphoreType.DMA((2, 6)),
        ],
        compiler_params=pltpu.CompilerParams(
            collective_id=0, has_side_effects=True, vmem_limit_bytes=60 * 2**20
        ),
        cost_estimate=pl.CostEstimate(
            flops=60 * 10**9, bytes_accessed=8 * 2**20, transcendentals=0
        ),
    )(
        index, cut_low, cut_high,
        previous.reshape(block), current.reshape(block), potential.reshape(ROWS, LANES),
        projector.reshape(NBLK, NPROJ, LANES), node_index.reshape(NBLK, LANES), coupling,
    )
    return following.reshape(shape), last.reshape(shape)


def solution(mesh):
    placed = (
        P(None, "gx", "gy", "gz"),
        P(None, "gx", "gy", "gz"),
        P("gx", "gy", "gz"),
        P("gx", "gy", "gz", None, None, None, None),
        P("gx", "gy", "gz", None, None, None),
        P(("gx", "gy", "gz"), None, None),
        P(),
        P(),
    )
    return jax.shard_map(
        shards,
        mesh=mesh,
        in_specs=placed,
        out_specs=(P(None, "gx", "gy", "gz"), P(None, "gx", "gy", "gz")),
        check_vma=False,
    )
```

```python
import jax
import jax.numpy as jnp
from jax import lax
from jax.experimental import pallas as pl
from jax.experimental.pallas import tpu as pltpu
from jax.sharding import PartitionSpec as P

F32 = jnp.float32
BF16 = jnp.bfloat16
MESH = pl.DeviceIdType.MESH

BANDS = 16
ROWS = 128
LANES = 128
LINE = 16
PLANES = 8
NOFF = 27
ATOMS = 4
SHARE = 2
NPROJ = 18
PPAD = 32
PSEND = 24
HALF = ROWS // 2
CENTRE = NOFF // 2
TRIO = 3
NCHUNK = NOFF // TRIO
BLOCKS = TRIO * SHARE
WIDE = BLOCKS * LANES
DEEP = BLOCKS * PPAD
GROUP = SHARE * BANDS
OTHERS = [offset for offset in range(NOFF) if offset != CENTRE]


def split(value):
    high = value.astype(BF16)
    return high, (value - high.astype(F32)).astype(BF16)


def kernel(
    sizes,
    low_s, high_s,
    previous, current, potential, projector, index_v, coupling,
    following, last,
    onehot, proj_hi, proj_lo, halved, held, spreads, coup,
    send_c, recv_c, send_w, recv_w,
    face_y, face_z, halo_x, halo_y, halo_z,
    sem_sc, sem_rc, sem_sw, sem_rw, sem_sh, sem_rh,
):
    place = tuple(lax.axis_index(axis) for axis in ("gx", "gy", "gz"))
    centre = 0.5 * (high_s[0] + low_s[0])
    radius = 0.5 * (high_s[0] - low_s[0])
    scale = 2.0 / radius

    around = [
        (lax.rem(at + count - 1, count), at, lax.rem(at + 1, count))
        for at, count in zip(place, sizes)
    ]
    exists = [(at > 0, None, at < count - 1) for at, count in zip(place, sizes)]

    def shift_of(offset):
        return offset // 9 - 1, (offset // 3) % 3 - 1, offset % 3 - 1

    def towards(offset, sign):
        return tuple(
            around[axis][sign * step + 1] for axis, step in enumerate(shift_of(offset))
        )

    def inside(offset, sign):
        valid = None
        for axis, step in enumerate(shift_of(offset)):
            here = exists[axis][sign * step + 1]
            if here is not None:
                valid = here if valid is None else valid & here
        return valid

    barrier = pltpu.get_barrier_semaphore()

    for offset in OTHERS:
        pl.semaphore_signal(
            barrier, inc=1, device_id=towards(offset, 1), device_id_type=MESH
        )

    lane_of = lambda rows: lax.broadcasted_iota(jnp.int32, (rows, LANES), 1)
    row_of = lambda rows: lax.broadcasted_iota(jnp.int32, (rows, LANES), 0)

    def prepare(offset, carry):
        wide = lax.broadcasted_iota(jnp.int32, (2 * LANES, LANES), 0)
        for atom in range(ATOMS):
            block = (atom // SHARE * NOFF + offset) * SHARE + atom % SHARE
            values = jnp.concatenate(
                [projector[offset, :, atom, :], jnp.zeros((PPAD - NPROJ, LANES), F32)], axis=0
            )
            high, low = split(values)
            at = pl.ds(pl.multiple_of(block * PPAD, PPAD), PPAD)
            proj_hi[at, :] = high
            proj_lo[at, :] = low
            node = index_v[offset, atom:atom + 1, :]
            column = (node // (HALF * LANES)) * LANES + node % LANES
            onehot[:, pl.ds(pl.multiple_of(block * LANES, LANES), LANES)] = jnp.where(
                wide == column, 1.0, 0.0
            ).astype(BF16)
        return carry

    lax.fori_loop(0, NOFF, prepare, 0)

    coup[...] = jnp.zeros(coup.shape, F32)
    for atom in range(ATOMS):
        coup[atom * PPAD:atom * PPAD + NPROJ, 0:NPROJ] = coupling[:, atom, :]
    held[...] = jnp.zeros(held.shape, F32)
    proj_hi[ATOMS * NOFF * PPAD:, :] = jnp.zeros((SHARE * PPAD, LANES), BF16)
    proj_lo[ATOMS * NOFF * PPAD:, :] = jnp.zeros((SHARE * PPAD, LANES), BF16)

    sides = [(axis, sign) for axis in range(3) for sign in (1, -1)]

    def neighbour(axis, sign):
        return tuple(
            around[n][sign + 1] if n == axis else at for n, at in enumerate(place)
        )

    def halo_copies(step, field):
        copies = []
        for n, (axis, sign) in enumerate(sides):
            slot = 0 if sign == 1 else 1
            if axis == 0:
                source = field.at[:, pl.ds(ROWS - LINE if sign == 1 else 0, LINE), :]
                target = halo_x.at[step, slot]
            elif axis == 1:
                source, target = face_y.at[step, slot], halo_y.at[step, slot]
            else:
                source, target = face_z.at[step, slot], halo_z.at[step, slot]
            copies.append(
                pltpu.make_async_remote_copy(
                    src_ref=source, dst_ref=target,
                    send_sem=sem_sh.at[step, n], recv_sem=sem_rh.at[step, n],
                    device_id=neighbour(axis, sign), device_id_type=MESH,
                )
            )
        return copies

    def part_copy(unit, offset):
        return pltpu.make_async_remote_copy(
            src_ref=send_c.at[unit, offset], dst_ref=recv_c.at[unit, offset],
            send_sem=sem_sc.at[unit, offset], recv_sem=sem_rc.at[unit, offset],
            device_id=towards(offset, 1), device_id_type=MESH,
        )

    def weight_copy(unit, offset):
        return pltpu.make_async_remote_copy(
            src_ref=send_w.at[unit], dst_ref=recv_w.at[unit, offset],
            send_sem=sem_sw.at[unit, offset], recv_sem=sem_rw.at[unit, offset],
            device_id=towards(offset, -1), device_id_type=MESH,
        )

    third = lane_of(8) // GROUP

    def turned(value, groups):
        shift = groups * GROUP % LANES
        return pltpu.roll(value, shift, 1) if shift else value

    def row_mask(share, chunk, block):
        atom = share * SHARE + block % SHARE
        node = index_v[chunk * TRIO + block // SHARE, atom:atom + 1, :]
        return (node // LANES) % HALF == row_of(HALF)

    def contract(unit, share, chunk, slot, into):
        first = (share * NCHUNK + chunk) * DEEP
        at = pl.ds(pl.multiple_of(first, DEEP), DEEP)
        p_hi, p_lo = proj_hi[at, :], proj_lo[at, :]
        high, low = split(held[slot])
        product = lax.dot_general(
            jnp.concatenate([p_hi, p_lo, p_hi], axis=1),
            jnp.concatenate([high, high, low], axis=1),
            (((1,), (1,)), ((), ())),
            preferred_element_type=F32,
        )
        tile = jnp.zeros((PSEND, LANES), F32)
        for k in range(BLOCKS):
            tile = jnp.where(
                lane_of(PSEND) // BANDS == k, product[k * PPAD:k * PPAD + PSEND], tile
            )
        for n in range(TRIO):
            message = jnp.zeros((8, LANES), F32)
            for p in range(3):
                message = jnp.where(third == p, turned(tile[8 * p:8 * p + 8], p - n), message)
            send_c[unit, into * TRIO + n] = message

    def gather(unit, share, special, action):
        def body(chunk, carry):
            slot = lax.rem(chunk, 2)
            contract(
                unit, share, jnp.maximum(chunk - 1, 0), 1 - slot,
                lax.rem(chunk + NCHUNK, NCHUNK + 1),
            )
            for two in range(BLOCKS // 2):
                first = (share * NCHUNK + chunk) * WIDE + two * 2 * LANES
                columns = onehot[:, pl.ds(pl.multiple_of(first, 2 * LANES), 2 * LANES)]
                product = jnp.dot(
                    halved[...], jnp.concatenate([columns, columns], axis=0),
                    preferred_element_type=F32,
                )
                for n in range(2):
                    block = two * 2 + n
                    mine = product[:, n * LANES:(n + 1) * LANES].reshape(BANDS, HALF, LANES)
                    held[slot, block * BANDS:(block + 1) * BANDS, :] = jnp.sum(
                        jnp.where(row_mask(share, chunk, block)[None], mine, 0.0), axis=1
                    )
            if action is not None:
                pl.when(chunk == special)(action)
            return carry

        lax.fori_loop(0, NCHUNK, body, 0)
        contract(unit, share, NCHUNK - 1, (NCHUNK - 1) % 2, NCHUNK - 1)

    def couple(unit, share):
        total = send_c[unit, CENTRE]
        for offset in OTHERS:
            part_copy(unit, offset).wait()
            total = total + jnp.where(inside(offset, -1), recv_c[unit, offset], 0.0)
        total = jnp.concatenate(
            [turned(total, -p) for p in range(3)]
            + [jnp.zeros((LANES - PSEND, LANES), F32)], axis=0
        )
        product = jnp.dot(
            coup[share * SHARE * PPAD:(share + 1) * SHARE * PPAD, :], total, precision=lax.Precision.HIGHEST, preferred_element_type=F32
        )
        weighted = jnp.zeros((PSEND, LANES), F32)
        for atom in range(SHARE):
            weighted = jnp.where(
                lane_of(PSEND) // BANDS == atom,
                product[atom * PPAD:atom * PPAD + PSEND], weighted,
            )
        message = jnp.zeros((8, LANES), F32)
        for p in range(3):
            message = jnp.where(third == p, turned(weighted[8 * p:8 * p + 8], p), message)
        send_w[unit] = scale * message
        recv_w[unit, CENTRE] = scale * message
        for offset in OTHERS:
            weight_copy(unit, offset).start()

    def spread(unit, share, chunk, slot):
        received = [recv_w[unit, chunk * TRIO + n] for n in range(TRIO)]
        rows = []
        for p in range(3):
            row = jnp.zeros((8, LANES), F32)
            for n in range(TRIO):
                row = jnp.where(third == n, turned(received[n], n - p), row)
            rows.append(row)
        rows.append(jnp.zeros((PPAD - PSEND, LANES), F32))
        weights = jnp.concatenate(rows * (LANES // PPAD), axis=0).T
        owner = row_of(LANES) // BANDS - lane_of(LANES) // PPAD
        weights = jnp.concatenate(
            [jnp.where(owner == n * (LANES // PPAD), weights, 0.0) for n in range(2)], axis=1
        )
        high, low = split(weights)
        first = (share * NCHUNK + chunk) * DEEP
        at = pl.ds(pl.multiple_of(first, DEEP), 2 * LANES)
        p_hi, p_lo = proj_hi[at, :], proj_lo[at, :]
        spreads[slot] = jnp.dot(
            jnp.concatenate([high, low, high], axis=1),
            jnp.concatenate([p_hi, p_hi, p_lo], axis=0),
            preferred_element_type=F32,
        )

    def scatter(unit, share, result, special, action):
        def body(chunk, carry):
            high, low = split(spreads[chunk])
            parts_hi, parts_lo = [], []
            for block in range(BLOCKS):
                mask = row_mask(share, chunk, block)
                for value, parts in ((high, parts_hi), (low, parts_lo)):
                    mine = value[block * BANDS:(block + 1) * BANDS].astype(F32)
                    parts.append(
                        jnp.where(mask[None], mine[:, None, :], 0.0)
                        .astype(BF16).reshape(BANDS * HALF, LANES)
                    )
            first = (share * NCHUNK + chunk) * WIDE
            columns = onehot[:, pl.ds(pl.multiple_of(first, WIDE), WIDE)]
            product = lax.dot_general(
                jnp.concatenate(parts_hi + parts_lo, axis=1),
                jnp.concatenate([columns, columns], axis=1),
                (((1,), (1,)), ((), ())),
                preferred_element_type=F32,
            )
            product = product.reshape(BANDS, HALF, 2 * LANES)
            result[:, 0:HALF, :] += product[:, :, 0:LANES]
            result[:, HALF:ROWS, :] += product[:, :, LANES:]
            if action is not None:
                pl.when(chunk == special)(action)
            return carry

        for offset in OTHERS:
            weight_copy(unit, offset).wait()
            recv_w[unit, offset] = jnp.where(inside(offset, 1), recv_w[unit, offset], 0.0)
        def ahead(n, carry):
            for m in range(3):
                spread(unit, share, n * 3 + m, n * 3 + m)
            return carry

        lax.fori_loop(0, NCHUNK // 3, ahead, 0)
        lax.fori_loop(0, NCHUNK, body, 0, unroll=3)

    def advance(step, before, field, result):
        face_y[step, 0] = field[:, pl.ds(LINE - 1, PLANES, stride=LINE), :]
        face_y[step, 1] = field[:, pl.ds(0, PLANES, stride=LINE), :]
        top = jnp.zeros((ROWS, LANES), F32)
        bottom = jnp.zeros((ROWS, LANES), F32)
        lanes = lane_of(ROWS)
        for band in range(BANDS):
            plane = field[band]
            top = jnp.where(lanes == band, pltpu.roll(plane, band + 1, 1), top)
            bottom = jnp.where(
                lanes == band, pltpu.roll(plane, band, 1) if band else plane, bottom
            )
        face_z[step, 0] = top
        face_z[step, 1] = bottom
        def cut(band, carry):
            at = pl.ds(pl.multiple_of(band * HALF, HALF), HALF)
            high, low = split(field[band])
            for half in range(2):
                rows = slice(half * HALF, (half + 1) * HALF)
                halved[at, half * LANES:(half + 1) * LANES] = high[rows]
                halved[at, (2 + half) * LANES:(3 + half) * LANES] = low[rows]
            return carry

        lax.fori_loop(0, BANDS, cut, 0)

        first, second = 2 * step, 2 * step + 1
        halos = halo_copies(step, field)
        if step > 0:
            for copy in halos:
                copy.start()
        gather(first, 0, 0, None)
        if step == 0:
            pl.semaphore_wait(barrier, len(OTHERS))
            for copy in halos:
                copy.start()
        for offset in OTHERS:
            part_copy(first, offset).start()
        gather(second, 1, 5, lambda: couple(first, 0))
        for offset in OTHERS:
            part_copy(second, offset).start()

        for copy in halos:
            copy.wait()
        edge = [(exists[axis][0], exists[axis][2]) for axis in range(3)]
        zside = [
            jnp.where(edge[2][slot], halo_z[step, slot], 0.0) for slot in range(2)
        ]

        line_of = lax.broadcasted_iota(jnp.int32, (PLANES, LINE, LANES), 1)
        def stencil(band):
            plane = field[band]
            below_x = jnp.where(edge[0][0], halo_x[step, 0, band], 0.0)
            above_x = jnp.where(edge[0][1], halo_x[step, 1, band], 0.0)
            beside = jnp.concatenate([below_x, plane[:ROWS - LINE]], axis=0)
            beside = beside + jnp.concatenate([plane[LINE:], above_x], axis=0)
            below_y = jnp.where(edge[1][0], halo_y[step, 0, band], 0.0)
            above_y = jnp.where(edge[1][1], halo_y[step, 1, band], 0.0)
            down = pltpu.roll(plane, 1, 0).reshape(PLANES, LINE, LANES)
            up = pltpu.roll(plane, ROWS - 1, 0).reshape(PLANES, LINE, LANES)
            down = jnp.where(line_of == 0, below_y[:, None, :], down)
            up = jnp.where(line_of == LINE - 1, above_y[:, None, :], up)
            beside = beside + (down + up).reshape(ROWS, LANES)
            back = pltpu.roll(plane, 1, 1)
            ahead = pltpu.roll(plane, LANES - 1, 1)
            side_b = pltpu.roll(zside[0], (LANES - band) % LANES, 1) if band else zside[0]
            side_a = pltpu.roll(zside[1], LANES - 1 - band, 1)
            back = jnp.where(lanes == 0, side_b, back)
            ahead = jnp.where(lanes == LANES - 1, side_a, ahead)
            beside = beside + (back + ahead)
            local = 0.5 * (6.0 * plane - beside) + (potential[...] - centre) * plane
            result[band] = scale * local - before[band]

        for band in range(BANDS):
            stencil(band)

        scatter(first, 0, result, 3, lambda: couple(second, 1))
        scatter(second, 1, result, 0, None)

    advance(0, previous, current, following)
    advance(1, current, following, last)


def shards(previous, current, potential, projector, node_index, coupling, cut_low, cut_high):
    sizes = tuple(lax.axis_size(axis) for axis in ("gx", "gy", "gz"))
    shape = current.shape
    block = (BANDS, ROWS, LANES)
    vmem = pl.BlockSpec(memory_space=pltpu.VMEM)
    smem = pl.BlockSpec(memory_space=pltpu.SMEM)
    index = node_index.reshape(NOFF, ATOMS, LANES)

    def body(*refs):
        kernel(sizes, *refs)

    following, last = pl.pallas_call(
        body,
        out_shape=[jax.ShapeDtypeStruct(block, F32)] * 2,
        in_specs=[smem] * 2 + [vmem] * 6,
        out_specs=[vmem, vmem],
        scratch_shapes=[
            pltpu.VMEM((2 * LANES, NOFF * ATOMS * LANES), BF16),
            pltpu.VMEM(((NOFF * ATOMS + SHARE) * PPAD, LANES), BF16),
            pltpu.VMEM(((NOFF * ATOMS + SHARE) * PPAD, LANES), BF16),
            pltpu.VMEM((BANDS * HALF, 4 * LANES), BF16),
            pltpu.VMEM((2, LANES, LANES), F32),
            pltpu.VMEM((NCHUNK, LANES, LANES), F32),
            pltpu.VMEM((ATOMS * PPAD, LANES), F32),
            pltpu.VMEM((4, NOFF + TRIO, 8, LANES), F32),
            pltpu.VMEM((4, NOFF, 8, LANES), F32),
            pltpu.VMEM((4, 8, LANES), F32),
            pltpu.VMEM((4, NOFF, 8, LANES), F32),
            pltpu.VMEM((2, 2, BANDS, PLANES, LANES), F32),
            pltpu.VMEM((2, 2, ROWS, LANES), F32),
            pltpu.VMEM((2, 2, BANDS, LINE, LANES), F32),
            pltpu.VMEM((2, 2, BANDS, PLANES, LANES), F32),
            pltpu.VMEM((2, 2, ROWS, LANES), F32),
            pltpu.SemaphoreType.DMA((4, NOFF)),
            pltpu.SemaphoreType.DMA((4, NOFF)),
            pltpu.SemaphoreType.DMA((4, NOFF)),
            pltpu.SemaphoreType.DMA((4, NOFF)),
            pltpu.SemaphoreType.DMA((2, 6)),
            pltpu.SemaphoreType.DMA((2, 6)),
        ],
        compiler_params=pltpu.CompilerParams(
            collective_id=0, has_side_effects=True, vmem_limit_bytes=60 * 2**20
        ),
        cost_estimate=pl.CostEstimate(
            flops=60 * 10**9, bytes_accessed=8 * 2**20, transcendentals=0
        ),
    )(
        cut_low, cut_high,
        previous.reshape(block), current.reshape(block), potential.reshape(ROWS, LANES),
        jnp.swapaxes(projector.reshape(NOFF, ATOMS, NPROJ, LANES), 1, 2), index,
        jnp.swapaxes(coupling, 0, 1),
    )
    return following.reshape(shape), last.reshape(shape)


def solution(mesh):
    placed = (
        P(None, "gx", "gy", "gz"),
        P(None, "gx", "gy", "gz"),
        P("gx", "gy", "gz"),
        P("gx", "gy", "gz", None, None, None, None),
        P("gx", "gy", "gz", None, None, None),
        P(("gx", "gy", "gz"), None, None),
        P(),
        P(),
    )
    return jax.shard_map(
        shards,
        mesh=mesh,
        in_specs=placed,
        out_specs=(P(None, "gx", "gy", "gz"), P(None, "gx", "gy", "gz")),
        check_vma=False,
    )
```

```python
import jax
import jax.numpy as jnp
from jax import lax
from jax.experimental import pallas as pl
from jax.experimental.pallas import tpu as pltpu
from jax.sharding import PartitionSpec as P

F32 = jnp.float32
BF16 = jnp.bfloat16
MESH = pl.DeviceIdType.MESH

BANDS = 16
ROWS = 128
LANES = 128
LINE = 16
PLANES = 8
NOFF = 27
ATOMS = 4
SHARE = 2
NPROJ = 18
PPAD = 32
PSEND = 24
HALF = ROWS // 2
CENTRE = NOFF // 2
TRIO = 3
NCHUNK = NOFF // TRIO
BLOCKS = TRIO * SHARE
WIDE = BLOCKS * LANES
DEEP = BLOCKS * PPAD
GROUP = SHARE * BANDS
OTHERS = [offset for offset in range(NOFF) if offset != CENTRE]


def split(value):
    high = value.astype(BF16)
    return high, (value - high.astype(F32)).astype(BF16)


def kernel(
    sizes,
    low_s, high_s,
    previous, current, potential, projector, index_v, coupling,
    following, last,
    onehot, proj_hi, proj_lo, halved, held, spreads, coup,
    send_c, recv_c, send_w, recv_w,
    face_y, face_z, halo_x, halo_y, halo_z,
    sem_sc, sem_rc, sem_sw, sem_rw, sem_sh, sem_rh,
):
    place = tuple(lax.axis_index(axis) for axis in ("gx", "gy", "gz"))
    centre = 0.5 * (high_s[0] + low_s[0])
    radius = 0.5 * (high_s[0] - low_s[0])
    scale = 2.0 / radius

    around = [
        (lax.rem(at + count - 1, count), at, lax.rem(at + 1, count))
        for at, count in zip(place, sizes)
    ]
    exists = [(at > 0, None, at < count - 1) for at, count in zip(place, sizes)]

    def shift_of(offset):
        return offset // 9 - 1, (offset // 3) % 3 - 1, offset % 3 - 1

    def towards(offset, sign):
        return tuple(
            around[axis][sign * step + 1] for axis, step in enumerate(shift_of(offset))
        )

    def inside(offset, sign):
        valid = None
        for axis, step in enumerate(shift_of(offset)):
            here = exists[axis][sign * step + 1]
            if here is not None:
                valid = here if valid is None else valid & here
        return valid

    barrier = pltpu.get_barrier_semaphore()

    for offset in OTHERS:
        pl.semaphore_signal(
            barrier, inc=1, device_id=towards(offset, 1), device_id_type=MESH
        )

    lane_of = lambda rows: lax.broadcasted_iota(jnp.int32, (rows, LANES), 1)
    row_of = lambda rows: lax.broadcasted_iota(jnp.int32, (rows, LANES), 0)

    def prepare(offset, carry):
        wide = lax.broadcasted_iota(jnp.int32, (2 * LANES, LANES), 0)
        for atom in range(ATOMS):
            block = (atom // SHARE * NOFF + offset) * SHARE + atom % SHARE
            values = jnp.concatenate(
                [projector[offset, :, atom, :], jnp.zeros((PPAD - NPROJ, LANES), F32)], axis=0
            )
            high, low = split(values)
            at = pl.ds(pl.multiple_of(block * PPAD, PPAD), PPAD)
            proj_hi[at, :] = high
            proj_lo[at, :] = low
            node = index_v[offset, atom:atom + 1, :]
            column = (node // (HALF * LANES)) * LANES + node % LANES
            onehot[:, pl.ds(pl.multiple_of(block * LANES, LANES), LANES)] = jnp.where(
                wide == column, 1.0, 0.0
            ).astype(BF16)
        return carry

    lax.fori_loop(0, NOFF, prepare, 0)

    coup[...] = jnp.zeros(coup.shape, F32)
    for atom in range(ATOMS):
        coup[atom * PPAD:atom * PPAD + NPROJ, 0:NPROJ] = coupling[:, atom, :]
    held[...] = jnp.zeros(held.shape, F32)
    proj_hi[ATOMS * NOFF * PPAD:, :] = jnp.zeros((SHARE * PPAD, LANES), BF16)
    proj_lo[ATOMS * NOFF * PPAD:, :] = jnp.zeros((SHARE * PPAD, LANES), BF16)

    sides = [(axis, sign) for axis in range(3) for sign in (1, -1)]

    def neighbour(axis, sign):
        return tuple(
            around[n][sign + 1] if n == axis else at for n, at in enumerate(place)
        )

    def halo_copies(step, field):
        copies = []
        for n, (axis, sign) in enumerate(sides):
            slot = 0 if sign == 1 else 1
            if axis == 0:
                source = field.at[:, pl.ds(ROWS - LINE if sign == 1 else 0, LINE), :]
                target = halo_x.at[step, slot]
            elif axis == 1:
                source, target = face_y.at[step, slot], halo_y.at[step, slot]
            else:
                source, target = face_z.at[step, slot], halo_z.at[step, slot]
            copies.append(
                pltpu.make_async_remote_copy(
                    src_ref=source, dst_ref=target,
                    send_sem=sem_sh.at[step, n], recv_sem=sem_rh.at[step, n],
                    device_id=neighbour(axis, sign), device_id_type=MESH,
                )
            )
        return copies

    def part_copy(unit, offset):
        return pltpu.make_async_remote_copy(
            src_ref=send_c.at[unit, offset], dst_ref=recv_c.at[unit, offset],
            send_sem=sem_sc.at[unit, offset], recv_sem=sem_rc.at[unit, offset],
            device_id=towards(offset, 1), device_id_type=MESH,
        )

    def weight_copy(unit, offset):
        return pltpu.make_async_remote_copy(
            src_ref=send_w.at[unit], dst_ref=recv_w.at[unit, offset],
            send_sem=sem_sw.at[unit, offset], recv_sem=sem_rw.at[unit, offset],
            device_id=towards(offset, -1), device_id_type=MESH,
        )

    third = lane_of(8) // GROUP

    def turned(value, groups):
        shift = groups * GROUP % LANES
        return pltpu.roll(value, shift, 1) if shift else value

    def row_mask(share, chunk, block):
        atom = share * SHARE + block % SHARE
        node = index_v[chunk * TRIO + block // SHARE, atom:atom + 1, :]
        return (node // LANES) % HALF == row_of(HALF)

    def contract(unit, share, chunk, slot, into):
        first = (share * NCHUNK + chunk) * DEEP
        at = pl.ds(pl.multiple_of(first, DEEP), DEEP)
        p_hi, p_lo = proj_hi[at, :], proj_lo[at, :]
        high, low = split(held[slot])
        product = lax.dot_general(
            jnp.concatenate([p_hi, p_lo, p_hi], axis=1),
            jnp.concatenate([high, high, low], axis=1),
            (((1,), (1,)), ((), ())),
            preferred_element_type=F32,
        )
        tile = jnp.zeros((PSEND, LANES), F32)
        for k in range(BLOCKS):
            tile = jnp.where(
                lane_of(PSEND) // BANDS == k, product[k * PPAD:k * PPAD + PSEND], tile
            )
        for n in range(TRIO):
            message = jnp.zeros((8, LANES), F32)
            for p in range(3):
                message = jnp.where(third == p, turned(tile[8 * p:8 * p + 8], p - n), message)
            send_c[unit, into * TRIO + n] = message

    def gather(unit, share, special, action):
        def body(chunk, carry):
            slot = lax.rem(chunk, 2)
            contract(
                unit, share, jnp.maximum(chunk - 1, 0), 1 - slot,
                lax.rem(chunk + NCHUNK, NCHUNK + 1),
            )
            for two in range(BLOCKS // 2):
                first = (share * NCHUNK + chunk) * WIDE + two * 2 * LANES
                columns = onehot[:, pl.ds(pl.multiple_of(first, 2 * LANES), 2 * LANES)]
                product = jnp.dot(
                    halved[...], jnp.concatenate([columns, columns], axis=0),
                    preferred_element_type=F32,
                )
                for n in range(2):
                    block = two * 2 + n
                    mine = product[:, n * LANES:(n + 1) * LANES].reshape(BANDS, HALF, LANES)
                    held[slot, block * BANDS:(block + 1) * BANDS, :] = jnp.sum(
                        jnp.where(row_mask(share, chunk, block)[None], mine, 0.0), axis=1
                    )
            if action is not None:
                pl.when(chunk == special)(action)
            return carry

        lax.fori_loop(0, NCHUNK, body, 0)
        contract(unit, share, NCHUNK - 1, (NCHUNK - 1) % 2, NCHUNK - 1)

    def couple(unit, share):
        total = send_c[unit, CENTRE]
        for offset in OTHERS:
            part_copy(unit, offset).wait()
            total = total + jnp.where(inside(offset, -1), recv_c[unit, offset], 0.0)
        total = jnp.concatenate(
            [turned(total, -p) for p in range(3)]
            + [jnp.zeros((LANES - PSEND, LANES), F32)], axis=0
        )
        product = jnp.dot(
            coup[share * SHARE * PPAD:(share + 1) * SHARE * PPAD, :], total, precision=lax.Precision.HIGHEST, preferred_element_type=F32
        )
        weighted = jnp.zeros((PSEND, LANES), F32)
        for atom in range(SHARE):
            weighted = jnp.where(
                lane_of(PSEND) // BANDS == atom,
                product[atom * PPAD:atom * PPAD + PSEND], weighted,
            )
        message = jnp.zeros((8, LANES), F32)
        for p in range(3):
            message = jnp.where(third == p, turned(weighted[8 * p:8 * p + 8], p), message)
        send_w[unit] = scale * message
        recv_w[unit, CENTRE] = scale * message
        for offset in OTHERS:
            weight_copy(unit, offset).start()

    def spread(unit, share, chunk, slot):
        received = [recv_w[unit, chunk * TRIO + n] for n in range(TRIO)]
        rows = []
        for p in range(3):
            row = jnp.zeros((8, LANES), F32)
            for n in range(TRIO):
                row = jnp.where(third == n, turned(received[n], n - p), row)
            rows.append(row)
        rows.append(jnp.zeros((PPAD - PSEND, LANES), F32))
        weights = jnp.concatenate(rows * (LANES // PPAD), axis=0).T
        owner = row_of(LANES) // BANDS - lane_of(LANES) // PPAD
        weights = jnp.concatenate(
            [jnp.where(owner == n * (LANES // PPAD), weights, 0.0) for n in range(2)], axis=1
        )
        high, low = split(weights)
        first = (share * NCHUNK + chunk) * DEEP
        at = pl.ds(pl.multiple_of(first, DEEP), 2 * LANES)
        p_hi, p_lo = proj_hi[at, :], proj_lo[at, :]
        spreads[slot] = jnp.dot(
            jnp.concatenate([high, low, high], axis=1),
            jnp.concatenate([p_hi, p_hi, p_lo], axis=0),
            preferred_element_type=F32,
        )

    def scatter(unit, share, result, special, action):
        def body(turn, carry):
            parts_hi, parts_lo = [], []
            for m in range(3):
                chunk = turn * 3 + m
                high, low = split(spreads[chunk])
                for block in range(BLOCKS):
                    mask = row_mask(share, chunk, block)
                    for value, parts in ((high, parts_hi), (low, parts_lo)):
                        mine = value[block * BANDS:(block + 1) * BANDS].astype(F32)
                        parts.append(
                            jnp.where(mask[None], mine[:, None, :], 0.0)
                            .astype(BF16).reshape(BANDS * HALF, LANES)
                        )
            width = 3 * WIDE
            first = share * NCHUNK * WIDE + turn * width
            columns = onehot[:, pl.ds(pl.multiple_of(first, width), width)]
            product = lax.dot_general(
                jnp.concatenate(parts_hi + parts_lo, axis=1),
                jnp.concatenate([columns, columns], axis=1),
                (((1,), (1,)), ((), ())),
                preferred_element_type=F32,
            )
            product = product.reshape(BANDS, HALF, 2 * LANES)
            result[:, 0:HALF, :] += product[:, :, 0:LANES]
            result[:, HALF:ROWS, :] += product[:, :, LANES:]
            if action is not None:
                pl.when(turn == special)(action)
            return carry

        for offset in OTHERS:
            weight_copy(unit, offset).wait()
            recv_w[unit, offset] = jnp.where(inside(offset, 1), recv_w[unit, offset], 0.0)
        def ahead(n, carry):
            for m in range(3):
                spread(unit, share, n * 3 + m, n * 3 + m)
            return carry

        lax.fori_loop(0, NCHUNK // 3, ahead, 0)
        lax.fori_loop(0, NCHUNK // 3, body, 0)

    def advance(step, before, field, result):
        face_y[step, 0] = field[:, pl.ds(LINE - 1, PLANES, stride=LINE), :]
        face_y[step, 1] = field[:, pl.ds(0, PLANES, stride=LINE), :]
        top = jnp.zeros((ROWS, LANES), F32)
        bottom = jnp.zeros((ROWS, LANES), F32)
        lanes = lane_of(ROWS)
        for band in range(BANDS):
            plane = field[band]
            top = jnp.where(lanes == band, pltpu.roll(plane, band + 1, 1), top)
            bottom = jnp.where(
                lanes == band, pltpu.roll(plane, band, 1) if band else plane, bottom
            )
        face_z[step, 0] = top
        face_z[step, 1] = bottom
        def cut(band, carry):
            at = pl.ds(pl.multiple_of(band * HALF, HALF), HALF)
            high, low = split(field[band])
            for half in range(2):
                rows = slice(half * HALF, (half + 1) * HALF)
                halved[at, half * LANES:(half + 1) * LANES] = high[rows]
                halved[at, (2 + half) * LANES:(3 + half) * LANES] = low[rows]
            return carry

        lax.fori_loop(0, BANDS, cut, 0)

        first, second = 2 * step, 2 * step + 1
        halos = halo_copies(step, field)
        if step > 0:
            for copy in halos:
                copy.start()
        gather(first, 0, 0, None)
        if step == 0:
            pl.semaphore_wait(barrier, len(OTHERS))
            for copy in halos:
                copy.start()
        for offset in OTHERS:
            part_copy(first, offset).start()
        gather(second, 1, 5, lambda: couple(first, 0))
        for offset in OTHERS:
            part_copy(second, offset).start()

        for copy in halos:
            copy.wait()
        edge = [(exists[axis][0], exists[axis][2]) for axis in range(3)]
        zside = [
            jnp.where(edge[2][slot], halo_z[step, slot], 0.0) for slot in range(2)
        ]

        line_of = lax.broadcasted_iota(jnp.int32, (PLANES, LINE, LANES), 1)
        def stencil(band):
            plane = field[band]
            below_x = jnp.where(edge[0][0], halo_x[step, 0, band], 0.0)
            above_x = jnp.where(edge[0][1], halo_x[step, 1, band], 0.0)
            beside = jnp.concatenate([below_x, plane[:ROWS - LINE]], axis=0)
            beside = beside + jnp.concatenate([plane[LINE:], above_x], axis=0)
            below_y = jnp.where(edge[1][0], halo_y[step, 0, band], 0.0)
            above_y = jnp.where(edge[1][1], halo_y[step, 1, band], 0.0)
            down = pltpu.roll(plane, 1, 0).reshape(PLANES, LINE, LANES)
            up = pltpu.roll(plane, ROWS - 1, 0).reshape(PLANES, LINE, LANES)
            down = jnp.where(line_of == 0, below_y[:, None, :], down)
            up = jnp.where(line_of == LINE - 1, above_y[:, None, :], up)
            beside = beside + (down + up).reshape(ROWS, LANES)
            back = pltpu.roll(plane, 1, 1)
            ahead = pltpu.roll(plane, LANES - 1, 1)
            side_b = pltpu.roll(zside[0], (LANES - band) % LANES, 1) if band else zside[0]
            side_a = pltpu.roll(zside[1], LANES - 1 - band, 1)
            back = jnp.where(lanes == 0, side_b, back)
            ahead = jnp.where(lanes == LANES - 1, side_a, ahead)
            beside = beside + (back + ahead)
            local = 0.5 * (6.0 * plane - beside) + (potential[...] - centre) * plane
            result[band] = scale * local - before[band]

        for band in range(BANDS):
            stencil(band)

        scatter(first, 0, result, 1, lambda: couple(second, 1))
        scatter(second, 1, result, 0, None)

    advance(0, previous, current, following)
    advance(1, current, following, last)


def hand_on(first_in, second_in, first_out, second_out, sem):
    copies = []
    for n, (source, target) in enumerate(((first_in, first_out), (second_in, second_out))):
        for part in range(4):
            bands = pl.ds(part * (BANDS // 4), BANDS // 4)
            copies.append(
                pltpu.make_async_copy(source.at[bands], target.at[bands], sem.at[n, part])
            )
    for copy in copies:
        copy.start()
    for copy in copies:
        copy.wait()


def shards(previous, current, potential, projector, node_index, coupling, cut_low, cut_high):
    sizes = tuple(lax.axis_size(axis) for axis in ("gx", "gy", "gz"))
    shape = current.shape
    block = (BANDS, ROWS, LANES)
    vmem = pl.BlockSpec(memory_space=pltpu.VMEM)
    smem = pl.BlockSpec(memory_space=pltpu.SMEM)
    index = node_index.reshape(NOFF, ATOMS, LANES)

    def body(*refs):
        kernel(sizes, *refs)

    following, last = pl.pallas_call(
        body,
        out_shape=[jax.ShapeDtypeStruct(block, F32)] * 2,
        in_specs=[smem] * 2 + [vmem] * 6,
        out_specs=[vmem, vmem],
        scratch_shapes=[
            pltpu.VMEM((2 * LANES, NOFF * ATOMS * LANES), BF16),
            pltpu.VMEM(((NOFF * ATOMS + SHARE) * PPAD, LANES), BF16),
            pltpu.VMEM(((NOFF * ATOMS + SHARE) * PPAD, LANES), BF16),
            pltpu.VMEM((BANDS * HALF, 4 * LANES), BF16),
            pltpu.VMEM((2, LANES, LANES), F32),
            pltpu.VMEM((NCHUNK, LANES, LANES), F32),
            pltpu.VMEM((ATOMS * PPAD, LANES), F32),
            pltpu.VMEM((4, NOFF + TRIO, 8, LANES), F32),
            pltpu.VMEM((4, NOFF, 8, LANES), F32),
            pltpu.VMEM((4, 8, LANES), F32),
            pltpu.VMEM((4, NOFF, 8, LANES), F32),
            pltpu.VMEM((2, 2, BANDS, PLANES, LANES), F32),
            pltpu.VMEM((2, 2, ROWS, LANES), F32),
            pltpu.VMEM((2, 2, BANDS, LINE, LANES), F32),
            pltpu.VMEM((2, 2, BANDS, PLANES, LANES), F32),
            pltpu.VMEM((2, 2, ROWS, LANES), F32),
            pltpu.SemaphoreType.DMA((4, NOFF)),
            pltpu.SemaphoreType.DMA((4, NOFF)),
            pltpu.SemaphoreType.DMA((4, NOFF)),
            pltpu.SemaphoreType.DMA((4, NOFF)),
            pltpu.SemaphoreType.DMA((2, 6)),
            pltpu.SemaphoreType.DMA((2, 6)),
        ],
        compiler_params=pltpu.CompilerParams(
            collective_id=0, has_side_effects=True, vmem_limit_bytes=60 * 2**20
        ),
        cost_estimate=pl.CostEstimate(
            flops=60 * 10**9, bytes_accessed=8 * 2**20, transcendentals=0
        ),
    )(
        cut_low, cut_high,
        previous.reshape(block), current.reshape(block), potential.reshape(ROWS, LANES),
        jnp.swapaxes(projector.reshape(NOFF, ATOMS, NPROJ, LANES), 1, 2), index,
        jnp.swapaxes(coupling, 0, 1),
    )
    anywhere = pl.BlockSpec(memory_space=pl.ANY)
    following, last = pl.pallas_call(
        hand_on,
        out_shape=[jax.ShapeDtypeStruct(block, F32)] * 2,
        in_specs=[anywhere] * 2,
        out_specs=[anywhere] * 2,
        scratch_shapes=[pltpu.SemaphoreType.DMA((2, 4))],
        cost_estimate=pl.CostEstimate(flops=0, bytes_accessed=4 * 2**20, transcendentals=0),
    )(following, last)
    return following.reshape(shape), last.reshape(shape)


def solution(mesh):
    placed = (
        P(None, "gx", "gy", "gz"),
        P(None, "gx", "gy", "gz"),
        P("gx", "gy", "gz"),
        P("gx", "gy", "gz", None, None, None, None),
        P("gx", "gy", "gz", None, None, None),
        P(("gx", "gy", "gz"), None, None),
        P(),
        P(),
    )
    return jax.shard_map(
        shards,
        mesh=mesh,
        in_specs=placed,
        out_specs=(P(None, "gx", "gy", "gz"), P(None, "gx", "gy", "gz")),
        check_vma=False,
    )
```

```python
import jax
import jax.numpy as jnp
from jax import lax
from jax.experimental import pallas as pl
from jax.experimental.pallas import tpu as pltpu
from jax.sharding import PartitionSpec as P

F32 = jnp.float32
BF16 = jnp.bfloat16
MESH = pl.DeviceIdType.MESH

BANDS = 16
ROWS = 128
LANES = 128
LINE = 16
PLANES = 8
NOFF = 27
ATOMS = 4
SHARE = 2
NPROJ = 18
PPAD = 32
PSEND = 24
HALF = ROWS // 2
CENTRE = NOFF // 2
TRIO = 3
NCHUNK = NOFF // TRIO
BLOCKS = TRIO * SHARE
WIDE = BLOCKS * LANES
DEEP = BLOCKS * PPAD
GROUP = SHARE * BANDS
OTHERS = [offset for offset in range(NOFF) if offset != CENTRE]


def split(value):
    high = value.astype(BF16)
    return high, (value - high.astype(F32)).astype(BF16)


def kernel(
    sizes,
    low_s, high_s,
    previous, current, potential, projector, index_v, coupling,
    following, last,
    onehot, proj_hi, proj_lo, halved, held, spreads, coup,
    send_c, recv_c, send_w, recv_w,
    face_y, face_z, halo_x, halo_y, halo_z,
    sem_sc, sem_rc, sem_sw, sem_rw, sem_sh, sem_rh,
):
    place = tuple(lax.axis_index(axis) for axis in ("gx", "gy", "gz"))
    centre = 0.5 * (high_s[0] + low_s[0])
    radius = 0.5 * (high_s[0] - low_s[0])
    scale = 2.0 / radius

    around = [
        (lax.rem(at + count - 1, count), at, lax.rem(at + 1, count))
        for at, count in zip(place, sizes)
    ]
    exists = [(at > 0, None, at < count - 1) for at, count in zip(place, sizes)]

    def shift_of(offset):
        return offset // 9 - 1, (offset // 3) % 3 - 1, offset % 3 - 1

    def towards(offset, sign):
        return tuple(
            around[axis][sign * step + 1] for axis, step in enumerate(shift_of(offset))
        )

    def inside(offset, sign):
        valid = None
        for axis, step in enumerate(shift_of(offset)):
            here = exists[axis][sign * step + 1]
            if here is not None:
                valid = here if valid is None else valid & here
        return valid

    barrier = pltpu.get_barrier_semaphore()

    for offset in OTHERS:
        pl.semaphore_signal(
            barrier, inc=1, device_id=towards(offset, 1), device_id_type=MESH
        )

    lane_of = lambda rows: lax.broadcasted_iota(jnp.int32, (rows, LANES), 1)
    row_of = lambda rows: lax.broadcasted_iota(jnp.int32, (rows, LANES), 0)

    def prepare(offset, carry):
        wide = lax.broadcasted_iota(jnp.int32, (2 * LANES, LANES), 0)
        for atom in range(ATOMS):
            block = (atom // SHARE * NOFF + offset) * SHARE + atom % SHARE
            values = jnp.concatenate(
                [projector[offset, :, atom, :], jnp.zeros((PPAD - NPROJ, LANES), F32)], axis=0
            )
            high, low = split(values)
            at = pl.ds(pl.multiple_of(block * PPAD, PPAD), PPAD)
            proj_hi[at, :] = high
            proj_lo[at, :] = low
            node = index_v[offset, atom:atom + 1, :]
            column = (node // (HALF * LANES)) * LANES + node % LANES
            onehot[:, pl.ds(pl.multiple_of(block * LANES, LANES), LANES)] = jnp.where(
                wide == column, 1.0, 0.0
            ).astype(BF16)
        return carry

    lax.fori_loop(0, NOFF, prepare, 0)

    coup[...] = jnp.zeros(coup.shape, F32)
    for atom in range(ATOMS):
        coup[atom * PPAD:atom * PPAD + NPROJ, 0:NPROJ] = coupling[:, atom, :]
    held[...] = jnp.zeros(held.shape, F32)
    proj_hi[ATOMS * NOFF * PPAD:, :] = jnp.zeros((SHARE * PPAD, LANES), BF16)
    proj_lo[ATOMS * NOFF * PPAD:, :] = jnp.zeros((SHARE * PPAD, LANES), BF16)

    sides = [(axis, sign) for axis in range(3) for sign in (1, -1)]

    def neighbour(axis, sign):
        return tuple(
            around[n][sign + 1] if n == axis else at for n, at in enumerate(place)
        )

    def halo_copies(step, field):
        copies = []
        for n, (axis, sign) in enumerate(sides):
            slot = 0 if sign == 1 else 1
            if axis == 0:
                source = field.at[:, pl.ds(ROWS - LINE if sign == 1 else 0, LINE), :]
                target = halo_x.at[step, slot]
            elif axis == 1:
                source, target = face_y.at[step, slot], halo_y.at[step, slot]
            else:
                source, target = face_z.at[step, slot], halo_z.at[step, slot]
            copies.append(
                pltpu.make_async_remote_copy(
                    src_ref=source, dst_ref=target,
                    send_sem=sem_sh.at[step, n], recv_sem=sem_rh.at[step, n],
                    device_id=neighbour(axis, sign), device_id_type=MESH,
                )
            )
        return copies

    def part_copy(unit, offset):
        return pltpu.make_async_remote_copy(
            src_ref=send_c.at[unit, offset], dst_ref=recv_c.at[unit, offset],
            send_sem=sem_sc.at[unit, offset], recv_sem=sem_rc.at[unit, offset],
            device_id=towards(offset, 1), device_id_type=MESH,
        )

    def weight_copy(unit, offset):
        return pltpu.make_async_remote_copy(
            src_ref=send_w.at[unit], dst_ref=recv_w.at[unit, offset],
            send_sem=sem_sw.at[unit, offset], recv_sem=sem_rw.at[unit, offset],
            device_id=towards(offset, -1), device_id_type=MESH,
        )

    third = lane_of(8) // GROUP

    def turned(value, groups):
        shift = groups * GROUP % LANES
        return pltpu.roll(value, shift, 1) if shift else value

    def row_mask(share, chunk, block):
        atom = share * SHARE + block % SHARE
        node = index_v[chunk * TRIO + block // SHARE, atom:atom + 1, :]
        return (node // LANES) % HALF == row_of(HALF)

    def contract(unit, share, chunk, slot, into):
        first = (share * NCHUNK + chunk) * DEEP
        at = pl.ds(pl.multiple_of(first, DEEP), DEEP)
        p_hi, p_lo = proj_hi[at, :], proj_lo[at, :]
        high, low = split(held[slot])
        product = lax.dot_general(
            jnp.concatenate([p_hi, p_lo, p_hi], axis=1),
            jnp.concatenate([high, high, low], axis=1),
            (((1,), (1,)), ((), ())),
            preferred_element_type=F32,
        )
        tile = jnp.zeros((PSEND, LANES), F32)
        for k in range(BLOCKS):
            tile = jnp.where(
                lane_of(PSEND) // BANDS == k, product[k * PPAD:k * PPAD + PSEND], tile
            )
        for n in range(TRIO):
            message = jnp.zeros((8, LANES), F32)
            for p in range(3):
                message = jnp.where(third == p, turned(tile[8 * p:8 * p + 8], p - n), message)
            send_c[unit, into * TRIO + n] = message

    def gather(unit, share, special, action):
        def body(chunk, carry):
            slot = lax.rem(chunk, 2)
            contract(
                unit, share, jnp.maximum(chunk - 1, 0), 1 - slot,
                lax.rem(chunk + NCHUNK, NCHUNK + 1),
            )
            for two in range(BLOCKS // 2):
                first = (share * NCHUNK + chunk) * WIDE + two * 2 * LANES
                columns = onehot[:, pl.ds(pl.multiple_of(first, 2 * LANES), 2 * LANES)]
                product = jnp.dot(
                    halved[...], jnp.concatenate([columns, columns], axis=0),
                    preferred_element_type=F32,
                )
                for n in range(2):
                    block = two * 2 + n
                    mine = product[:, n * LANES:(n + 1) * LANES].reshape(BANDS, HALF, LANES)
                    held[slot, block * BANDS:(block + 1) * BANDS, :] = jnp.sum(
                        jnp.where(row_mask(share, chunk, block)[None], mine, 0.0), axis=1
                    )
            if action is not None:
                pl.when(chunk == special)(action)
            return carry

        lax.fori_loop(0, NCHUNK, body, 0)
        contract(unit, share, NCHUNK - 1, (NCHUNK - 1) % 2, NCHUNK - 1)

    def couple(unit, share):
        total = send_c[unit, CENTRE]
        for offset in OTHERS:
            part_copy(unit, offset).wait()
            total = total + jnp.where(inside(offset, -1), recv_c[unit, offset], 0.0)
        total = jnp.concatenate(
            [turned(total, -p) for p in range(3)]
            + [jnp.zeros((LANES - PSEND, LANES), F32)], axis=0
        )
        product = jnp.dot(
            coup[share * SHARE * PPAD:(share + 1) * SHARE * PPAD, :], total, precision=lax.Precision.HIGHEST, preferred_element_type=F32
        )
        weighted = jnp.zeros((PSEND, LANES), F32)
        for atom in range(SHARE):
            weighted = jnp.where(
                lane_of(PSEND) // BANDS == atom,
                product[atom * PPAD:atom * PPAD + PSEND], weighted,
            )
        message = jnp.zeros((8, LANES), F32)
        for p in range(3):
            message = jnp.where(third == p, turned(weighted[8 * p:8 * p + 8], p), message)
        send_w[unit] = scale * message
        recv_w[unit, CENTRE] = scale * message
        for offset in OTHERS:
            weight_copy(unit, offset).start()

    def spread(unit, share, chunk, slot):
        received = [recv_w[unit, chunk * TRIO + n] for n in range(TRIO)]
        rows = []
        for p in range(3):
            row = jnp.zeros((8, LANES), F32)
            for n in range(TRIO):
                row = jnp.where(third == n, turned(received[n], n - p), row)
            rows.append(row)
        rows.append(jnp.zeros((PPAD - PSEND, LANES), F32))
        weights = jnp.concatenate(rows * (LANES // PPAD), axis=0).T
        owner = row_of(LANES) // BANDS - lane_of(LANES) // PPAD
        weights = jnp.concatenate(
            [jnp.where(owner == n * (LANES // PPAD), weights, 0.0) for n in range(2)], axis=1
        )
        high, low = split(weights)
        first = (share * NCHUNK + chunk) * DEEP
        at = pl.ds(pl.multiple_of(first, DEEP), 2 * LANES)
        p_hi, p_lo = proj_hi[at, :], proj_lo[at, :]
        spreads[slot] = jnp.dot(
            jnp.concatenate([high, low, high], axis=1),
            jnp.concatenate([p_hi, p_hi, p_lo], axis=0),
            preferred_element_type=F32,
        )

    def scatter(unit, share, result, special, action):
        def body(turn, carry):
            parts_hi, parts_lo = [], []
            for m in range(3):
                chunk = turn * 3 + m
                high, low = split(spreads[chunk])
                for block in range(BLOCKS):
                    mask = row_mask(share, chunk, block)
                    for value, parts in ((high, parts_hi), (low, parts_lo)):
                        mine = value[block * BANDS:(block + 1) * BANDS].astype(F32)
                        parts.append(
                            jnp.where(mask[None], mine[:, None, :], 0.0)
                            .astype(BF16).reshape(BANDS * HALF, LANES)
                        )
            width = 3 * WIDE
            first = share * NCHUNK * WIDE + turn * width
            columns = onehot[:, pl.ds(pl.multiple_of(first, width), width)]
            product = lax.dot_general(
                jnp.concatenate(parts_hi + parts_lo, axis=1),
                jnp.concatenate([columns, columns], axis=1),
                (((1,), (1,)), ((), ())),
                preferred_element_type=F32,
            )
            product = product.reshape(BANDS, HALF, 2 * LANES)
            result[:, 0:HALF, :] += product[:, :, 0:LANES]
            result[:, HALF:ROWS, :] += product[:, :, LANES:]
            if action is not None:
                pl.when(turn == special)(action)
            return carry

        for offset in OTHERS:
            weight_copy(unit, offset).wait()
            recv_w[unit, offset] = jnp.where(inside(offset, 1), recv_w[unit, offset], 0.0)
        def ahead(n, carry):
            for m in range(3):
                spread(unit, share, n * 3 + m, n * 3 + m)
            return carry

        lax.fori_loop(0, NCHUNK // 3, ahead, 0)
        lax.fori_loop(0, NCHUNK // 3, body, 0)

    def advance(step, before, field, result):
        face_y[step, 0] = field[:, pl.ds(LINE - 1, PLANES, stride=LINE), :]
        face_y[step, 1] = field[:, pl.ds(0, PLANES, stride=LINE), :]
        top = jnp.zeros((ROWS, LANES), F32)
        bottom = jnp.zeros((ROWS, LANES), F32)
        lanes = lane_of(ROWS)
        for band in range(BANDS):
            plane = field[band]
            top = jnp.where(lanes == band, pltpu.roll(plane, band + 1, 1), top)
            bottom = jnp.where(
                lanes == band, pltpu.roll(plane, band, 1) if band else plane, bottom
            )
        face_z[step, 0] = top
        face_z[step, 1] = bottom
        def cut(band, carry):
            at = pl.ds(pl.multiple_of(band * HALF, HALF), HALF)
            high, low = split(field[band])
            for half in range(2):
                rows = slice(half * HALF, (half + 1) * HALF)
                halved[at, half * LANES:(half + 1) * LANES] = high[rows]
                halved[at, (2 + half) * LANES:(3 + half) * LANES] = low[rows]
            return carry

        lax.fori_loop(0, BANDS, cut, 0)

        first, second = 2 * step, 2 * step + 1
        halos = halo_copies(step, field)
        if step > 0:
            for copy in halos:
                copy.start()
        gather(first, 0, 0, None)
        if step == 0:
            pl.semaphore_wait(barrier, len(OTHERS))
            for copy in halos:
                copy.start()
        for offset in OTHERS:
            part_copy(first, offset).start()
        gather(second, 1, 5, lambda: couple(first, 0))
        for offset in OTHERS:
            part_copy(second, offset).start()

        for copy in halos:
            copy.wait()
        edge = [(exists[axis][0], exists[axis][2]) for axis in range(3)]
        zside = [
            jnp.where(edge[2][slot], halo_z[step, slot], 0.0) for slot in range(2)
        ]

        line_of = lax.broadcasted_iota(jnp.int32, (PLANES, LINE, LANES), 1)
        def stencil(band):
            plane = field[band]
            below_x = jnp.where(edge[0][0], halo_x[step, 0, band], 0.0)
            above_x = jnp.where(edge[0][1], halo_x[step, 1, band], 0.0)
            beside = jnp.concatenate([below_x, plane[:ROWS - LINE]], axis=0)
            beside = beside + jnp.concatenate([plane[LINE:], above_x], axis=0)
            below_y = jnp.where(edge[1][0], halo_y[step, 0, band], 0.0)
            above_y = jnp.where(edge[1][1], halo_y[step, 1, band], 0.0)
            down = pltpu.roll(plane, 1, 0).reshape(PLANES, LINE, LANES)
            up = pltpu.roll(plane, ROWS - 1, 0).reshape(PLANES, LINE, LANES)
            down = jnp.where(line_of == 0, below_y[:, None, :], down)
            up = jnp.where(line_of == LINE - 1, above_y[:, None, :], up)
            beside = beside + (down + up).reshape(ROWS, LANES)
            back = pltpu.roll(plane, 1, 1)
            ahead = pltpu.roll(plane, LANES - 1, 1)
            side_b = pltpu.roll(zside[0], (LANES - band) % LANES, 1) if band else zside[0]
            side_a = pltpu.roll(zside[1], LANES - 1 - band, 1)
            back = jnp.where(lanes == 0, side_b, back)
            ahead = jnp.where(lanes == LANES - 1, side_a, ahead)
            beside = beside + (back + ahead)
            local = 0.5 * (6.0 * plane - beside) + (potential[...] - centre) * plane
            result[band] = scale * local - before[band]

        for band in range(BANDS):
            stencil(band)

        scatter(first, 0, result, 1, lambda: couple(second, 1))
        scatter(second, 1, result, 0, None)

    advance(0, previous, current, following)
    advance(1, current, following, last)


def hand_on(first_in, second_in, first_out, second_out, first_held, second_held, sem_in, sem_out):
    coming, going = [], []
    for part in range(4):
        bands = pl.ds(part * (BANDS // 4), BANDS // 4)
        for n, (source, held, target) in enumerate(
            ((first_in, first_held, first_out), (second_in, second_held, second_out))
        ):
            coming.append(
                pltpu.make_async_copy(source.at[bands], held.at[bands], sem_in.at[n, part])
            )
            going.append(
                pltpu.make_async_copy(held.at[bands], target.at[bands], sem_out.at[n, part])
            )
    for copy in coming:
        copy.start()
    for here, there in zip(coming, going):
        here.wait()
        there.start()
    for copy in going:
        copy.wait()


def shards(previous, current, potential, projector, node_index, coupling, cut_low, cut_high):
    sizes = tuple(lax.axis_size(axis) for axis in ("gx", "gy", "gz"))
    shape = current.shape
    block = (BANDS, ROWS, LANES)
    vmem = pl.BlockSpec(memory_space=pltpu.VMEM)
    smem = pl.BlockSpec(memory_space=pltpu.SMEM)
    index = node_index.reshape(NOFF, ATOMS, LANES)

    def body(*refs):
        kernel(sizes, *refs)

    following, last = pl.pallas_call(
        body,
        out_shape=[jax.ShapeDtypeStruct(block, F32)] * 2,
        in_specs=[smem] * 2 + [vmem] * 6,
        out_specs=[vmem, vmem],
        scratch_shapes=[
            pltpu.VMEM((2 * LANES, NOFF * ATOMS * LANES), BF16),
            pltpu.VMEM(((NOFF * ATOMS + SHARE) * PPAD, LANES), BF16),
            pltpu.VMEM(((NOFF * ATOMS + SHARE) * PPAD, LANES), BF16),
            pltpu.VMEM((BANDS * HALF, 4 * LANES), BF16),
            pltpu.VMEM((2, LANES, LANES), F32),
            pltpu.VMEM((NCHUNK, LANES, LANES), F32),
            pltpu.VMEM((ATOMS * PPAD, LANES), F32),
            pltpu.VMEM((4, NOFF + TRIO, 8, LANES), F32),
            pltpu.VMEM((4, NOFF, 8, LANES), F32),
            pltpu.VMEM((4, 8, LANES), F32),
            pltpu.VMEM((4, NOFF, 8, LANES), F32),
            pltpu.VMEM((2, 2, BANDS, PLANES, LANES), F32),
            pltpu.VMEM((2, 2, ROWS, LANES), F32),
            pltpu.VMEM((2, 2, BANDS, LINE, LANES), F32),
            pltpu.VMEM((2, 2, BANDS, PLANES, LANES), F32),
            pltpu.VMEM((2, 2, ROWS, LANES), F32),
            pltpu.SemaphoreType.DMA((4, NOFF)),
            pltpu.SemaphoreType.DMA((4, NOFF)),
            pltpu.SemaphoreType.DMA((4, NOFF)),
            pltpu.SemaphoreType.DMA((4, NOFF)),
            pltpu.SemaphoreType.DMA((2, 6)),
            pltpu.SemaphoreType.DMA((2, 6)),
        ],
        compiler_params=pltpu.CompilerParams(
            collective_id=0, has_side_effects=True, vmem_limit_bytes=60 * 2**20
        ),
        cost_estimate=pl.CostEstimate(
            flops=60 * 10**9, bytes_accessed=8 * 2**20, transcendentals=0
        ),
    )(
        cut_low, cut_high,
        previous.reshape(block), current.reshape(block), potential.reshape(ROWS, LANES),
        jnp.swapaxes(projector.reshape(NOFF, ATOMS, NPROJ, LANES), 1, 2), index,
        jnp.swapaxes(coupling, 0, 1),
    )
    anywhere = pl.BlockSpec(memory_space=pl.ANY)
    following, last = pl.pallas_call(
        hand_on,
        out_shape=[jax.ShapeDtypeStruct(block, F32)] * 2,
        in_specs=[anywhere] * 2,
        out_specs=[anywhere] * 2,
        scratch_shapes=[
            pltpu.VMEM(block, F32),
            pltpu.VMEM(block, F32),
            pltpu.SemaphoreType.DMA((2, 4)),
            pltpu.SemaphoreType.DMA((2, 4)),
        ],
        cost_estimate=pl.CostEstimate(flops=0, bytes_accessed=4 * 2**20, transcendentals=0),
    )(following, last)
    return following.reshape(shape), last.reshape(shape)


def solution(mesh):
    placed = (
        P(None, "gx", "gy", "gz"),
        P(None, "gx", "gy", "gz"),
        P("gx", "gy", "gz"),
        P("gx", "gy", "gz", None, None, None, None),
        P("gx", "gy", "gz", None, None, None),
        P(("gx", "gy", "gz"), None, None),
        P(),
        P(),
    )
    return jax.shard_map(
        shards,
        mesh=mesh,
        in_specs=placed,
        out_specs=(P(None, "gx", "gy", "gz"), P(None, "gx", "gy", "gz")),
        check_vma=False,
    )
```

```python
import jax
import jax.numpy as jnp
from jax import lax
from jax.experimental import pallas as pl
from jax.experimental.pallas import tpu as pltpu
from jax.sharding import PartitionSpec as P

F32 = jnp.float32
BF16 = jnp.bfloat16
MESH = pl.DeviceIdType.MESH

BANDS = 16
ROWS = 128
LANES = 128
LINE = 16
PLANES = 8
NOFF = 27
ATOMS = 4
SHARE = 2
NPROJ = 18
PPAD = 32
PSEND = 24
HALF = ROWS // 2
CENTRE = NOFF // 2
TRIO = 3
NCHUNK = NOFF // TRIO
BLOCKS = TRIO * SHARE
WIDE = BLOCKS * LANES
DEEP = BLOCKS * PPAD
GROUP = SHARE * BANDS
OTHERS = [offset for offset in range(NOFF) if offset != CENTRE]


def split(value):
    high = value.astype(BF16)
    return high, (value - high.astype(F32)).astype(BF16)


def kernel(
    sizes,
    low_s, high_s,
    previous, current, potential, projector, index_v, coupling,
    following, last,
    onehot, proj_hi, proj_lo, halved, held, spreads, coup,
    send_c, recv_c, send_w, recv_w,
    face_y, face_z, halo_x, halo_y, halo_z,
    sem_sc, sem_rc, sem_sw, sem_rw, sem_sh, sem_rh,
):
    place = tuple(lax.axis_index(axis) for axis in ("gx", "gy", "gz"))
    centre = 0.5 * (high_s[0] + low_s[0])
    radius = 0.5 * (high_s[0] - low_s[0])
    scale = 2.0 / radius

    around = [
        (lax.rem(at + count - 1, count), at, lax.rem(at + 1, count))
        for at, count in zip(place, sizes)
    ]
    exists = [(at > 0, None, at < count - 1) for at, count in zip(place, sizes)]

    def shift_of(offset):
        return offset // 9 - 1, (offset // 3) % 3 - 1, offset % 3 - 1

    def towards(offset, sign):
        return tuple(
            around[axis][sign * step + 1] for axis, step in enumerate(shift_of(offset))
        )

    def inside(offset, sign):
        valid = None
        for axis, step in enumerate(shift_of(offset)):
            here = exists[axis][sign * step + 1]
            if here is not None:
                valid = here if valid is None else valid & here
        return valid

    barrier = pltpu.get_barrier_semaphore()

    for offset in OTHERS:
        pl.semaphore_signal(
            barrier, inc=1, device_id=towards(offset, 1), device_id_type=MESH
        )

    lane_of = lambda rows: lax.broadcasted_iota(jnp.int32, (rows, LANES), 1)
    row_of = lambda rows: lax.broadcasted_iota(jnp.int32, (rows, LANES), 0)

    def prepare(offset, carry):
        wide = lax.broadcasted_iota(jnp.int32, (2 * LANES, LANES), 0)
        for atom in range(ATOMS):
            block = (atom // SHARE * NOFF + offset) * SHARE + atom % SHARE
            values = jnp.concatenate(
                [projector[offset, :, atom, :], jnp.zeros((PPAD - NPROJ, LANES), F32)], axis=0
            )
            high, low = split(values)
            at = pl.ds(pl.multiple_of(block * PPAD, PPAD), PPAD)
            proj_hi[at, :] = high
            proj_lo[at, :] = low
            node = index_v[offset, atom:atom + 1, :]
            column = (node // (HALF * LANES)) * LANES + node % LANES
            onehot[:, pl.ds(pl.multiple_of(block * LANES, LANES), LANES)] = jnp.where(
                wide == column, 1.0, 0.0
            ).astype(BF16)
        return carry

    lax.fori_loop(0, NOFF, prepare, 0)

    coup[...] = jnp.zeros(coup.shape, F32)
    for atom in range(ATOMS):
        coup[atom * PPAD:atom * PPAD + NPROJ, 0:NPROJ] = coupling[:, atom, :]
    held[...] = jnp.zeros(held.shape, F32)
    proj_hi[ATOMS * NOFF * PPAD:, :] = jnp.zeros((SHARE * PPAD, LANES), BF16)
    proj_lo[ATOMS * NOFF * PPAD:, :] = jnp.zeros((SHARE * PPAD, LANES), BF16)

    sides = [(axis, sign) for axis in range(3) for sign in (1, -1)]

    def neighbour(axis, sign):
        return tuple(
            around[n][sign + 1] if n == axis else at for n, at in enumerate(place)
        )

    def halo_copies(step, field):
        copies = []
        for n, (axis, sign) in enumerate(sides):
            slot = 0 if sign == 1 else 1
            if axis == 0:
                source = field.at[:, pl.ds(ROWS - LINE if sign == 1 else 0, LINE), :]
                target = halo_x.at[step, slot]
            elif axis == 1:
                source, target = face_y.at[step, slot], halo_y.at[step, slot]
            else:
                source, target = face_z.at[step, slot], halo_z.at[step, slot]
            copies.append(
                pltpu.make_async_remote_copy(
                    src_ref=source, dst_ref=target,
                    send_sem=sem_sh.at[step, n], recv_sem=sem_rh.at[step, n],
                    device_id=neighbour(axis, sign), device_id_type=MESH,
                )
            )
        return copies

    def part_copy(unit, offset):
        return pltpu.make_async_remote_copy(
            src_ref=send_c.at[unit, offset], dst_ref=recv_c.at[unit, offset],
            send_sem=sem_sc.at[unit, offset], recv_sem=sem_rc.at[unit, offset],
            device_id=towards(offset, 1), device_id_type=MESH,
        )

    def weight_copy(unit, offset):
        return pltpu.make_async_remote_copy(
            src_ref=send_w.at[unit], dst_ref=recv_w.at[unit, offset],
            send_sem=sem_sw.at[unit, offset], recv_sem=sem_rw.at[unit, offset],
            device_id=towards(offset, -1), device_id_type=MESH,
        )

    third = lane_of(8) // GROUP

    def turned(value, groups):
        shift = groups * GROUP % LANES
        return pltpu.roll(value, shift, 1) if shift else value

    def row_mask(share, chunk, block):
        atom = share * SHARE + block % SHARE
        node = index_v[chunk * TRIO + block // SHARE, atom:atom + 1, :]
        return (node // LANES) % HALF == row_of(HALF)

    def contract(unit, share, chunk, slot, into):
        first = (share * NCHUNK + chunk) * DEEP
        at = pl.ds(pl.multiple_of(first, DEEP), DEEP)
        p_hi, p_lo = proj_hi[at, :], proj_lo[at, :]
        high, low = split(held[slot])
        product = lax.dot_general(
            jnp.concatenate([p_hi, p_lo, p_hi], axis=1),
            jnp.concatenate([high, high, low], axis=1),
            (((1,), (1,)), ((), ())),
            preferred_element_type=F32,
        )
        tile = jnp.zeros((PSEND, LANES), F32)
        for k in range(BLOCKS):
            tile = jnp.where(
                lane_of(PSEND) // BANDS == k, product[k * PPAD:k * PPAD + PSEND], tile
            )
        for n in range(TRIO):
            message = jnp.zeros((8, LANES), F32)
            for p in range(3):
                message = jnp.where(third == p, turned(tile[8 * p:8 * p + 8], p - n), message)
            send_c[unit, into * TRIO + n] = message

    def gather(unit, share, special, action):
        def body(chunk, carry):
            slot = lax.rem(chunk, 2)
            contract(
                unit, share, jnp.maximum(chunk - 1, 0), 1 - slot,
                lax.rem(chunk + NCHUNK, NCHUNK + 1),
            )
            for two in range(BLOCKS // 2):
                first = (share * NCHUNK + chunk) * WIDE + two * 2 * LANES
                columns = onehot[:, pl.ds(pl.multiple_of(first, 2 * LANES), 2 * LANES)]
                product = jnp.dot(
                    halved[...], jnp.concatenate([columns, columns], axis=0),
                    preferred_element_type=F32,
                )
                for n in range(2):
                    block = two * 2 + n
                    mine = product[:, n * LANES:(n + 1) * LANES].reshape(BANDS, HALF, LANES)
                    held[slot, block * BANDS:(block + 1) * BANDS, :] = jnp.sum(
                        jnp.where(row_mask(share, chunk, block)[None], mine, 0.0), axis=1
                    )
            if action is not None:
                pl.when(chunk == special)(action)
            return carry

        lax.fori_loop(0, NCHUNK, body, 0)
        contract(unit, share, NCHUNK - 1, (NCHUNK - 1) % 2, NCHUNK - 1)

    def couple(unit, share):
        total = send_c[unit, CENTRE]
        for offset in OTHERS:
            part_copy(unit, offset).wait()
            total = total + jnp.where(inside(offset, -1), recv_c[unit, offset], 0.0)
        total = jnp.concatenate(
            [turned(total, -p) for p in range(3)]
            + [jnp.zeros((LANES - PSEND, LANES), F32)], axis=0
        )
        product = jnp.dot(
            coup[share * SHARE * PPAD:(share + 1) * SHARE * PPAD, :], total, precision=lax.Precision.HIGHEST, preferred_element_type=F32
        )
        weighted = jnp.zeros((PSEND, LANES), F32)
        for atom in range(SHARE):
            weighted = jnp.where(
                lane_of(PSEND) // BANDS == atom,
                product[atom * PPAD:atom * PPAD + PSEND], weighted,
            )
        message = jnp.zeros((8, LANES), F32)
        for p in range(3):
            message = jnp.where(third == p, turned(weighted[8 * p:8 * p + 8], p), message)
        send_w[unit] = scale * message
        recv_w[unit, CENTRE] = scale * message
        for offset in OTHERS:
            weight_copy(unit, offset).start()

    def spread(unit, share, chunk, slot):
        received = [recv_w[unit, chunk * TRIO + n] for n in range(TRIO)]
        rows = []
        for p in range(3):
            row = jnp.zeros((8, LANES), F32)
            for n in range(TRIO):
                row = jnp.where(third == n, turned(received[n], n - p), row)
            rows.append(row)
        rows.append(jnp.zeros((PPAD - PSEND, LANES), F32))
        weights = jnp.concatenate(rows * (LANES // PPAD), axis=0).T
        owner = row_of(LANES) // BANDS - lane_of(LANES) // PPAD
        weights = jnp.concatenate(
            [jnp.where(owner == n * (LANES // PPAD), weights, 0.0) for n in range(2)], axis=1
        )
        high, low = split(weights)
        first = (share * NCHUNK + chunk) * DEEP
        at = pl.ds(pl.multiple_of(first, DEEP), 2 * LANES)
        p_hi, p_lo = proj_hi[at, :], proj_lo[at, :]
        spreads[slot] = jnp.dot(
            jnp.concatenate([high, low, high], axis=1),
            jnp.concatenate([p_hi, p_hi, p_lo], axis=0),
            preferred_element_type=F32,
        )

    def scatter(unit, share, result, special, action):
        def body(turn, carry):
            parts_hi, parts_lo = [], []
            for m in range(3):
                chunk = turn * 3 + m
                high, low = split(spreads[chunk])
                for block in range(BLOCKS):
                    mask = row_mask(share, chunk, block)
                    for value, parts in ((high, parts_hi), (low, parts_lo)):
                        mine = value[block * BANDS:(block + 1) * BANDS].astype(F32)
                        parts.append(
                            jnp.where(mask[None], mine[:, None, :], 0.0)
                            .astype(BF16).reshape(BANDS * HALF, LANES)
                        )
            width = 3 * WIDE
            first = share * NCHUNK * WIDE + turn * width
            columns = onehot[:, pl.ds(pl.multiple_of(first, width), width)]
            product = lax.dot_general(
                jnp.concatenate(parts_hi + parts_lo, axis=1),
                jnp.concatenate([columns, columns], axis=1),
                (((1,), (1,)), ((), ())),
                preferred_element_type=F32,
            )
            product = product.reshape(BANDS, HALF, 2 * LANES)
            result[:, 0:HALF, :] += product[:, :, 0:LANES]
            result[:, HALF:ROWS, :] += product[:, :, LANES:]
            if action is not None:
                pl.when(turn == special)(action)
            return carry

        for offset in OTHERS:
            weight_copy(unit, offset).wait()
            recv_w[unit, offset] = jnp.where(inside(offset, 1), recv_w[unit, offset], 0.0)
        def ahead(n, carry):
            for m in range(3):
                spread(unit, share, n * 3 + m, n * 3 + m)
            return carry

        lax.fori_loop(0, NCHUNK // 3, ahead, 0)
        lax.fori_loop(0, NCHUNK // 3, body, 0)

    def advance(step, before, field, result):
        face_y[step, 0] = field[:, pl.ds(LINE - 1, PLANES, stride=LINE), :]
        face_y[step, 1] = field[:, pl.ds(0, PLANES, stride=LINE), :]
        top = jnp.zeros((ROWS, LANES), F32)
        bottom = jnp.zeros((ROWS, LANES), F32)
        lanes = lane_of(ROWS)
        for band in range(BANDS):
            plane = field[band]
            top = jnp.where(lanes == band, pltpu.roll(plane, band + 1, 1), top)
            bottom = jnp.where(
                lanes == band, pltpu.roll(plane, band, 1) if band else plane, bottom
            )
        face_z[step, 0] = top
        face_z[step, 1] = bottom
        def cut(band, carry):
            at = pl.ds(pl.multiple_of(band * HALF, HALF), HALF)
            high, low = split(field[band])
            for half in range(2):
                rows = slice(half * HALF, (half + 1) * HALF)
                halved[at, half * LANES:(half + 1) * LANES] = high[rows]
                halved[at, (2 + half) * LANES:(3 + half) * LANES] = low[rows]
            return carry

        lax.fori_loop(0, BANDS, cut, 0)

        first, second = 2 * step, 2 * step + 1
        halos = halo_copies(step, field)
        if step > 0:
            for copy in halos:
                copy.start()
        gather(first, 0, 0, None)
        if step == 0:
            pl.semaphore_wait(barrier, len(OTHERS))
            for copy in halos:
                copy.start()
        for offset in OTHERS:
            part_copy(first, offset).start()
        gather(second, 1, 5, lambda: couple(first, 0))
        for offset in OTHERS:
            part_copy(second, offset).start()

        for copy in halos:
            copy.wait()
        edge = [(exists[axis][0], exists[axis][2]) for axis in range(3)]
        zside = [
            jnp.where(edge[2][slot], halo_z[step, slot], 0.0) for slot in range(2)
        ]

        line_of = lax.broadcasted_iota(jnp.int32, (PLANES, LINE, LANES), 1)
        def stencil(band):
            plane = field[band]
            below_x = jnp.where(edge[0][0], halo_x[step, 0, band], 0.0)
            above_x = jnp.where(edge[0][1], halo_x[step, 1, band], 0.0)
            beside = jnp.concatenate([below_x, plane[:ROWS - LINE]], axis=0)
            beside = beside + jnp.concatenate([plane[LINE:], above_x], axis=0)
            below_y = jnp.where(edge[1][0], halo_y[step, 0, band], 0.0)
            above_y = jnp.where(edge[1][1], halo_y[step, 1, band], 0.0)
            down = pltpu.roll(plane, 1, 0).reshape(PLANES, LINE, LANES)
            up = pltpu.roll(plane, ROWS - 1, 0).reshape(PLANES, LINE, LANES)
            down = jnp.where(line_of == 0, below_y[:, None, :], down)
            up = jnp.where(line_of == LINE - 1, above_y[:, None, :], up)
            beside = beside + (down + up).reshape(ROWS, LANES)
            back = pltpu.roll(plane, 1, 1)
            ahead = pltpu.roll(plane, LANES - 1, 1)
            side_b = pltpu.roll(zside[0], (LANES - band) % LANES, 1) if band else zside[0]
            side_a = pltpu.roll(zside[1], LANES - 1 - band, 1)
            back = jnp.where(lanes == 0, side_b, back)
            ahead = jnp.where(lanes == LANES - 1, side_a, ahead)
            beside = beside + (back + ahead)
            local = 0.5 * (6.0 * plane - beside) + (potential[...] - centre) * plane
            result[band] = scale * local - before[band]

        for band in range(BANDS):
            stencil(band)

        scatter(first, 0, result, 0, lambda: couple(second, 1))
        scatter(second, 1, result, 0, None)

    advance(0, previous, current, following)
    advance(1, current, following, last)


def hand_on(first_in, second_in, first_out, second_out, first_held, second_held, sem_in, sem_out):
    coming, going = [], []
    for part in range(4):
        bands = pl.ds(part * (BANDS // 4), BANDS // 4)
        for n, (source, held, target) in enumerate(
            ((first_in, first_held, first_out), (second_in, second_held, second_out))
        ):
            coming.append(
                pltpu.make_async_copy(source.at[bands], held.at[bands], sem_in.at[n, part])
            )
            going.append(
                pltpu.make_async_copy(held.at[bands], target.at[bands], sem_out.at[n, part])
            )
    for copy in coming:
        copy.start()
    for here, there in zip(coming, going):
        here.wait()
        there.start()
    for copy in going:
        copy.wait()


def shards(previous, current, potential, projector, node_index, coupling, cut_low, cut_high):
    sizes = tuple(lax.axis_size(axis) for axis in ("gx", "gy", "gz"))
    shape = current.shape
    block = (BANDS, ROWS, LANES)
    vmem = pl.BlockSpec(memory_space=pltpu.VMEM)
    smem = pl.BlockSpec(memory_space=pltpu.SMEM)
    index = node_index.reshape(NOFF, ATOMS, LANES)

    def body(*refs):
        kernel(sizes, *refs)

    following, last = pl.pallas_call(
        body,
        out_shape=[jax.ShapeDtypeStruct(block, F32)] * 2,
        in_specs=[smem] * 2 + [vmem] * 6,
        out_specs=[vmem, vmem],
        scratch_shapes=[
            pltpu.VMEM((2 * LANES, NOFF * ATOMS * LANES), BF16),
            pltpu.VMEM(((NOFF * ATOMS + SHARE) * PPAD, LANES), BF16),
            pltpu.VMEM(((NOFF * ATOMS + SHARE) * PPAD, LANES), BF16),
            pltpu.VMEM((BANDS * HALF, 4 * LANES), BF16),
            pltpu.VMEM((2, LANES, LANES), F32),
            pltpu.VMEM((NCHUNK, LANES, LANES), F32),
            pltpu.VMEM((ATOMS * PPAD, LANES), F32),
            pltpu.VMEM((4, NOFF + TRIO, 8, LANES), F32),
            pltpu.VMEM((4, NOFF, 8, LANES), F32),
            pltpu.VMEM((4, 8, LANES), F32),
            pltpu.VMEM((4, NOFF, 8, LANES), F32),
            pltpu.VMEM((2, 2, BANDS, PLANES, LANES), F32),
            pltpu.VMEM((2, 2, ROWS, LANES), F32),
            pltpu.VMEM((2, 2, BANDS, LINE, LANES), F32),
            pltpu.VMEM((2, 2, BANDS, PLANES, LANES), F32),
            pltpu.VMEM((2, 2, ROWS, LANES), F32),
            pltpu.SemaphoreType.DMA((4, NOFF)),
            pltpu.SemaphoreType.DMA((4, NOFF)),
            pltpu.SemaphoreType.DMA((4, NOFF)),
            pltpu.SemaphoreType.DMA((4, NOFF)),
            pltpu.SemaphoreType.DMA((2, 6)),
            pltpu.SemaphoreType.DMA((2, 6)),
        ],
        compiler_params=pltpu.CompilerParams(
            collective_id=0, has_side_effects=True, vmem_limit_bytes=60 * 2**20
        ),
        cost_estimate=pl.CostEstimate(
            flops=60 * 10**9, bytes_accessed=8 * 2**20, transcendentals=0
        ),
    )(
        cut_low, cut_high,
        previous.reshape(block), current.reshape(block), potential.reshape(ROWS, LANES),
        jnp.swapaxes(projector.reshape(NOFF, ATOMS, NPROJ, LANES), 1, 2), index,
        jnp.swapaxes(coupling, 0, 1),
    )
    anywhere = pl.BlockSpec(memory_space=pl.ANY)
    following, last = pl.pallas_call(
        hand_on,
        out_shape=[jax.ShapeDtypeStruct(block, F32)] * 2,
        in_specs=[anywhere] * 2,
        out_specs=[anywhere] * 2,
        scratch_shapes=[
            pltpu.VMEM(block, F32),
            pltpu.VMEM(block, F32),
            pltpu.SemaphoreType.DMA((2, 4)),
            pltpu.SemaphoreType.DMA((2, 4)),
        ],
        cost_estimate=pl.CostEstimate(flops=0, bytes_accessed=4 * 2**20, transcendentals=0),
    )(following, last)
    return following.reshape(shape), last.reshape(shape)


def solution(mesh):
    placed = (
        P(None, "gx", "gy", "gz"),
        P(None, "gx", "gy", "gz"),
        P("gx", "gy", "gz"),
        P("gx", "gy", "gz", None, None, None, None),
        P("gx", "gy", "gz", None, None, None),
        P(("gx", "gy", "gz"), None, None),
        P(),
        P(),
    )
    return jax.shard_map(
        shards,
        mesh=mesh,
        in_specs=placed,
        out_specs=(P(None, "gx", "gy", "gz"), P(None, "gx", "gy", "gz")),
        check_vma=False,
    )
```
